256 devices in a mesh: gx: 8 (over y, core), gy: 32 (over x, z).
Axes of the slice: x: 4, y: 4, z: 8, core: 2. Of those that a mesh axis runs over, the one named last changes fastest.
Arguments:
- adjoint_fields: float32 [32, 256, 16, 512], P('gx', 'gy'), may hold values from -20 to 20
- center_coef: float32 [3, 32, 256, 16], P(None, 'gx', 'gy'), may hold values from -3 to -1.5
- neighbor_coef: float32 [3, 6, 32, 256, 16], P(None, None, 'gx', 'gy'), may hold values from 0.25 to 1
- neutral: float32 [32, 256, 16], P('gx', 'gy'), may hold values from -20 to 20
Outputs:
- orthonormal: float32 [32, 256, 16, 512], P('gx', 'gy')
- factor: float32 [512, 512], replicated
The draws below stay inside these ranges and needn't reach their ends.
All inputs are finite; a program needn't handle non-finite values.
Results may differ from the reference program's by a relative error of at most 0.00016.
Values sent between devices are 32-bit elements; how exact they have to be, the bound alone decides.
A program may use at most 64 MiB of HBM per device.

```python
import math
import jax
import jax.numpy as jnp
from jax import lax

M = 512
NZ = 16
STEPS = 2
LEVELS = 3
NX = 32
NY = 256


def neutral_base(key, exponent):
    key_rough, key_spread = jax.random.split(key)
    rough_part = jax.random.truncated_normal(key_rough, -4.0, 4.0, (NX, NY, NZ), jnp.float32)
    spread = jnp.exp(jax.random.uniform(key_spread, (NX, NY, NZ), jnp.float32, math.log(0.3), math.log(1.5)))
    coord_x = (jnp.arange(NX, dtype=jnp.float32) / NX)[:, None, None]
    coord_y = (jnp.arange(NY, dtype=jnp.float32) / NY)[None, :, None]
    ramp_scale = ((1.0 + 2.0 * coord_x) * (1.0 + 2.0 * coord_y) / 3.0) ** exponent
    return jnp.clip(rough_part * spread * ramp_scale, -20.0, 20.0)


def draw_neutral(key, part):
    shared = neutral_base(key, 1.0)
    return shared


def draw_adjoint_fields(key, part):
    shared = neutral_base(key, 1.0)
    key = jax.random.fold_in(key, 7)
    key_rough, key_beta = jax.random.split(key, 2)
    shape_all = (NX, NY, NZ, M)
    rough_part = jax.random.truncated_normal(key_rough, -4.0, 4.0, shape_all, jnp.float32)
    mixed_part = rough_part + 0.5 * jnp.roll(rough_part, 1, axis=3) + 0.3 * jnp.roll(rough_part, 37, axis=3)
    beta_weight = jax.random.uniform(key_beta, (M,), jnp.float32, -0.6, 0.6)
    combined = mixed_part + shared[..., None] * beta_weight
    return jnp.clip(combined, -20.0, 20.0)


def levels(stream_key, shape, shards, smallest, top_value):
    gain = 1.0
    for dim, blocks in shards:
        heights = jax.random.uniform(jax.random.fold_in(jax.random.fold_in(stream_key, 6), dim), (blocks,), jnp.float32, smallest / len(shards), top_value / len(shards))
        gain = gain * jnp.repeat(jnp.exp(heights), shape[dim] // blocks).reshape((-1,) + (1,) * (len(shape) - 1 - dim))
    return gain


def setup_inputs(seed: int = 0) -> dict:
    streams_of = jax.random.split(jax.random.key(seed), 5)
    return {
        "adjoint_fields": draw_adjoint_fields(jax.random.fold_in(streams_of[4], 71), 0),
        "center_coef": jnp.clip(-3.0 + 1.5 * jax.random.uniform(streams_of[1], (LEVELS, NX, NY, NZ), jnp.float32) ** levels(streams_of[1], (LEVELS, NX, NY, NZ), ((1, 8), (2, 32)), -0.2, 0.2), -3.0, -1.5),
        "neighbor_coef": jnp.clip(jnp.exp(math.log(1.0) - 1.3862944 * jax.random.uniform(streams_of[2], (LEVELS, 6, NX, NY, NZ), jnp.float32) ** levels(streams_of[2], (LEVELS, 6, NX, NY, NZ), ((2, 8), (3, 32)), -0.2, 0.2)), 0.25, 1.0),
        "neutral": draw_neutral(jax.random.fold_in(streams_of[4], 71), 0),
    }


STEP_SIZE = 0.15
EPSILON = 1e-06

def shift_depth(values, upward):
    padding = jnp.zeros_like(values[:, :, :1])
    if upward:
        return jnp.concatenate([padding, values[:, :, :-1]], axis=2)
    return jnp.concatenate([values[:, :, 1:], padding], axis=2)

def adjoint_apply(field_padded, coef_padded, margin):
    extent_x = field_padded.shape[0] - 2
    extent_y = field_padded.shape[1] - 2
    offset = 2 - margin

    def coef_at(component, step_x, step_y):
        return coef_padded[component, offset + step_x:offset + step_x + extent_x, offset + step_y:offset + step_y + extent_y, :][..., None]

    def field_at(step_x, step_y):
        return field_padded[1 + step_x:1 + step_x + extent_x, 1 + step_y:1 + step_y + extent_y]
    middle = field_at(0, 0)
    result = coef_at(0, 0, 0) * middle
    result = result + coef_at(1, -1, 0) * field_at(-1, 0)
    result = result + coef_at(2, 1, 0) * field_at(1, 0)
    result = result + coef_at(3, 0, -1) * field_at(0, -1)
    result = result + coef_at(4, 0, 1) * field_at(0, 1)
    result = result + shift_depth(coef_at(5, 0, 0) * middle, True)
    result = result + shift_depth(coef_at(6, 0, 0) * middle, False)
    return result

def pad_plane(values):
    return jnp.pad(values, ((1, 1), (1, 1), (0, 0), (0, 0)))

def evolve_block(block_field, coef_padded):
    adjoint_now = block_field
    for stepper in range(STEPS, 0, -1):
        slope_late = adjoint_apply(pad_plane(adjoint_now), coef_padded[stepper], 0)
        trial_field = adjoint_now + STEP_SIZE * slope_late
        slope_early = adjoint_apply(pad_plane(trial_field), coef_padded[stepper - 1], 0)
        adjoint_now = adjoint_now + 0.5 * STEP_SIZE * (slope_late + slope_early)
    return adjoint_now

def reference(adjoint_fields, center_coef, neighbor_coef, neutral):
    stacked = jnp.concatenate([center_coef[:, None], neighbor_coef], axis=1)
    coef_padded = jnp.pad(stacked, ((0, 0), (0, 0), (2, 2), (2, 2), (0, 0)))
    block_width = min(M, 128)
    grouped = adjoint_fields.reshape(NX, NY, NZ, M // block_width, block_width).transpose(3, 0, 1, 2, 4)

    def evolve(block_field):
        return evolve_block(block_field, coef_padded)
    evolved = lax.map(evolve, grouped).transpose(1, 2, 3, 0, 4).reshape(NX * NY * NZ, M)
    neutral_flat = neutral.reshape(-1)
    aligned = jnp.dot(neutral_flat, evolved, precision=lax.Precision.HIGHEST)
    squared = jnp.sum(neutral_flat * neutral_flat)
    weight = aligned / (squared + EPSILON)
    projected = evolved - neutral_flat[:, None] * weight[None, :]
    gram_matrix = jnp.dot(projected.T, projected, precision=lax.Precision.HIGHEST) / (NX * NY * NZ)
    factor = jnp.linalg.cholesky(gram_matrix)
    inverse = jax.scipy.linalg.solve_triangular(factor, jnp.eye(M, dtype=factor.dtype), lower=True)
    orthonormal = jnp.dot(projected, inverse.T, precision=lax.Precision.HIGHEST).reshape(NX, NY, NZ, M)
    return (orthonormal, factor)
```

```python
import functools

import jax
import jax.numpy as jnp
from jax import lax
from jax.experimental import pallas as pl
from jax.experimental.pallas import tpu as pltpu
from jax.sharding import PartitionSpec as P

STEP_SIZE = 0.15
EPSILON = 1e-06
HIGHEST = lax.Precision.HIGHEST


def dot_nt(a, b):
    return lax.dot_general(a, b, (((1,), (1,)), ((), ())), precision=HIGHEST,
                           preferred_element_type=jnp.float32)


def block_index(i, j):
    return i * (i + 1) // 2 + j


def lanes(value, column):
    return jnp.broadcast_to(value[:, column:column + 1], (8, 128))


def rows(value, row):
    return jnp.broadcast_to(value[row:row + 1, :], (8, 128))


def factor_diagonal(block_ref, upper_ref, inverse_ref):
    sub = lax.broadcasted_iota(jnp.int32, (8, 128), 0)
    lane = lax.broadcasted_iota(jnp.int32, (8, 128), 1)
    left = [block_ref[8 * i:8 * i + 8, :] for i in range(16)]
    right = [jnp.where(lane == sub + 8 * i, 1.0, 0.0).astype(jnp.float32) for i in range(16)]
    for k in range(16):
        base = 8 * k
        columns = [lanes(left[k], base + r) for r in range(8)]
        entry = {(q, r): rows(columns[r], q) for r in range(8) for q in range(r, 8)}
        u = [rows(left[k], r) for r in range(8)]
        v = [rows(right[k], r) for r in range(8)]
        scale = []
        lower = {}
        for r in range(8):
            s = lax.rsqrt(entry[r, r])
            scale.append(s)
            for q in range(r + 1, 8):
                lower[q, r] = entry[q, r] * s
            for q in range(r + 1, 8):
                for t in range(r + 1, q + 1):
                    entry[q, t] = entry[q, t] - lower[q, r] * lower[t, r]
            u[r] = u[r] * s
            v[r] = v[r] * s
            for q in range(r + 1, 8):
                u[q] = u[q] - lower[q, r] * u[r]
                v[q] = v[q] - lower[q, r] * v[r]
        for i in range(k + 1, 16):
            col = [lanes(left[i], base + r) for r in range(8)]
            for r in range(8):
                col[r] = col[r] * scale[r]
                for q in range(r + 1, 8):
                    col[q] = col[q] - lower[q, r] * col[r]
            for r in range(8):
                left[i] = left[i] - col[r] * u[r]
                right[i] = right[i] - col[r] * v[r]
        up = u[0]
        inv = v[0]
        for r in range(1, 8):
            up = jnp.where(sub == r, u[r], up)
            inv = jnp.where(sub == r, v[r], inv)
        upper_ref[base:base + 8, :] = jnp.where(lane >= sub + base, up, 0.0)
        inverse_ref[base:base + 8, :] = inv


def orthonormalize_kernel(cells, packed_ref, fields_ref, neutral_ref, out_ref, factor_ref,
                          gram, work, block, upper, inverse):
    nb = 4
    squared = packed_ref[160, 1:2, :]
    aligned = [packed_ref[160 + j, 0:1, :] for j in range(nb)]
    weight = [a / (squared + EPSILON) for a in aligned]
    ratio = jnp.sqrt(squared + 2 * EPSILON) / (squared + EPSILON)
    removed = [a * ratio for a in aligned]
    for i in range(nb):
        tall = jnp.broadcast_to(removed[i], (128, 128)).T
        for j in range(i + 1):
            b = block_index(i, j)
            raw = packed_ref[16 * b:16 * b + 16].reshape(128, 128)
            gram[128 * i:128 * i + 128, 128 * j:128 * j + 128] = (raw - tall * removed[j]) * (1.0 / cells)
    for j in range(nb):
        work[:, 128 * j:128 * j + 128] = fields_ref[:, 128 * j:128 * j + 128] - neutral_ref[...] * weight[j]
    for j in range(nb):
        here = pl.ds(128 * j, 128)
        block[...] = gram[here, here]
        factor_diagonal(block, upper, inverse)
        factor_ref[here, here] = upper[...].T
        inv = inverse[...]
        panels = {}
        for i in range(j + 1, nb):
            panels[i] = dot_nt(gram[128 * i:128 * i + 128, here], inv)
            factor_ref[128 * i:128 * i + 128, here] = panels[i]
            factor_ref[here, 128 * i:128 * i + 128] = jnp.zeros((128, 128), jnp.float32)
        q = dot_nt(work[:, here], inv)
        out_ref[:, here] = q
        for i in range(j + 1, nb):
            for k in range(j + 1, i + 1):
                there = pl.ds(128 * k, 128)
                gram[128 * i:128 * i + 128, there] = gram[128 * i:128 * i + 128, there] - dot_nt(panels[i], panels[k])
        for k in range(j + 1, nb):
            there = pl.ds(128 * k, 128)
            work[:, there] = work[:, there] - dot_nt(q, panels[k])


def orthonormalize(packed, fields, neutral_column, cells):
    n = fields.shape[0]
    vm = pl.BlockSpec(memory_space=pltpu.VMEM)
    return pl.pallas_call(
        functools.partial(orthonormalize_kernel, cells),
        out_shape=(jax.ShapeDtypeStruct((n, 512), jnp.float32), jax.ShapeDtypeStruct((512, 512), jnp.float32)),
        in_specs=[vm] * 3, out_specs=(vm, vm),
        scratch_shapes=[pltpu.VMEM((512, 512), jnp.float32), pltpu.VMEM((n, 512), jnp.float32),
                        pltpu.VMEM((128, 128), jnp.float32), pltpu.VMEM((128, 128), jnp.float32),
                        pltpu.VMEM((128, 128), jnp.float32)],
        compiler_params=pltpu.CompilerParams(vmem_limit_bytes=40 * 1024 * 1024),
    )(packed, fields, neutral_column)


MESH = pl.DeviceIdType.MESH
TILES = 192
CHUNK = 3


def reduce_kernel(fields_ref, neutral_ref, out_ref, pack, from_core, mid, from_first, low, from_second,
                  tail, from_third, core_sems, first_sems, second_sems, third_sems, back_sems):
    gx, gy = lax.axis_index("gx"), lax.axis_index("gy")
    core, y = lax.rem(gx, 2), lax.div(gx, 2)
    z, x = lax.rem(gy, 8), lax.div(gy, 8)
    other = 1 - core
    partner = (gx + 1 - 2 * core, gy)

    def along_y(step):
        peer = lax.rem(y + step, 4)
        return peer, (2 * peer + core, gy)

    def along_x(step):
        peer = lax.rem(x + step, 4)
        return peer, (gx, 8 * peer + z)

    def along_z(step):
        peer = lax.rem(z + step, 8)
        return peer, (gx, 8 * x + peer)

    barrier = pltpu.get_barrier_semaphore()
    pl.semaphore_signal(barrier, inc=1, device_id=partner, device_id_type=MESH)
    for step in range(1, 4):
        pl.semaphore_signal(barrier, inc=1, device_id=along_y(step)[1], device_id_type=MESH)
        pl.semaphore_signal(barrier, inc=1, device_id=along_x(step)[1], device_id_type=MESH)
    for step in range(1, 8):
        pl.semaphore_signal(barrier, inc=1, device_id=along_z(step)[1], device_id_type=MESH)

    for i in range(4):
        for j in range(i + 1):
            b = i * (i + 1) // 2 + j
            product = lax.dot_general(fields_ref[:, 128 * i:128 * i + 128], fields_ref[:, 128 * j:128 * j + 128],
                                      (((0,), (0,)), ((), ())), precision=HIGHEST,
                                      preferred_element_type=jnp.float32)
            pack[16 * b:16 * b + 16] = product.reshape(16, 8, 128)
    sub = lax.broadcasted_iota(jnp.int32, (8, 512), 0)
    row = neutral_ref[...]
    aligned = lax.dot_general(jnp.where(sub == 0, row, 0.0), fields_ref[...], (((1,), (0,)), ((), ())),
                              precision=HIGHEST, preferred_element_type=jnp.float32)
    extra = jnp.where(sub == 1, jnp.sum(row * row), aligned)
    for j in range(4):
        pack[160 + j] = extra[:, 128 * j:128 * j + 128]
    pack[164:TILES] = jnp.zeros((TILES - 164, 8, 128), jnp.float32)
    pl.semaphore_wait(barrier, 14)

    def copy(src, dst, sems, mine, theirs, device):
        return pltpu.make_async_remote_copy(src_ref=src, dst_ref=dst, send_sem=sems.at[0, theirs],
                                            recv_sem=sems.at[1, mine], device_id=device, device_id_type=MESH)

    half = TILES // 2
    quarter = half // 2
    piece = quarter // 4

    first = copy(pack.at[pl.ds(other * half, half)], from_core, core_sems, 0, 0, partner)
    first.start()
    first.wait()
    mid[...] = pack[pl.ds(core * half, half)] + from_core[...]

    started = []
    for step in range(1, 4):
        for h, (peer, device) in enumerate((along_y(step), along_x(step))):
            me = (y, x)[h]
            c = copy(mid.at[pl.ds(h * quarter + peer * piece, piece)], from_first.at[h, me], first_sems,
                     4 * h + me, 4 * h + peer, device)
            c.start()
            started.append((h, peer, device))
    for h in range(2):
        me = (y, x)[h]
        total = mid[pl.ds(h * quarter + me * piece, piece)]
        for g, peer, device in started:
            if g == h:
                c = copy(mid.at[pl.ds(h * quarter + peer * piece, piece)], from_first.at[h, peer], first_sems,
                         4 * h + peer, 4 * h + peer, device)
                c.wait()
                total = total + from_first[h, peer]
        low[h] = total
    started = []
    for step in range(1, 4):
        for h, (peer, device) in enumerate((along_x(step), along_y(step))):
            me = (x, y)[h]
            c = copy(low.at[h, pl.ds(peer * CHUNK, CHUNK)], from_second.at[h, me], second_sems,
                     4 * h + me, 4 * h + peer, device)
            c.start()
            started.append((h, peer, device))
    for h in range(2):
        me = (x, y)[h]
        total = low[h, pl.ds(me * CHUNK, CHUNK)]
        for g, peer, device in started:
            if g == h:
                c = copy(low.at[h, pl.ds(peer * CHUNK, CHUNK)], from_second.at[h, peer], second_sems,
                         4 * h + peer, 4 * h + peer, device)
                c.wait()
                total = total + from_second[h, peer]
        tail[h] = total
    started = []
    for step in range(1, 8):
        peer, device = along_z(step)
        c = copy(tail, from_third.at[z], third_sems, z, peer, device)
        c.start()
        started.append((peer, device))
    from_third[z] = tail[...]
    for peer, device in started:
        copy(tail, from_third.at[peer], third_sems, peer, peer, device).wait()
    final = from_third[0]
    for p in range(1, 8):
        final = final + from_third[p]

    own = core * half
    places = (own + y * piece + x * CHUNK, own + quarter + x * piece + y * CHUNK)
    for h in range(2):
        out_ref[pl.ds(places[h], CHUNK)] = final[h]
    started = []
    for step in range(1, 4):
        for h, (peer, device) in enumerate((along_x(step), along_y(step))):
            me = (x, y)[h]
            spot = out_ref.at[pl.ds(places[h], CHUNK)]
            copy(spot, spot, back_sems, 4 * h + me, 4 * h + peer, device).start()
            started.append((h, peer, device))
    for h, peer, device in started:
        place = (own + y * piece, own + quarter + x * piece)[h] + peer * CHUNK
        spot = out_ref.at[pl.ds(place, CHUNK)]
        copy(spot, spot, back_sems, 4 * h + peer, 4 * h + peer, device).wait()
    started = []
    for step in range(1, 4):
        for h, (peer, device) in enumerate((along_y(step), along_x(step))):
            me = (y, x)[h]
            spot = out_ref.at[pl.ds(own + h * quarter + me * piece, piece)]
            copy(spot, spot, back_sems, 8 + 4 * h + me, 8 + 4 * h + peer, device).start()
            started.append((h, peer, device))
    for h, peer, device in started:
        spot = out_ref.at[pl.ds(own + h * quarter + peer * piece, piece)]
        copy(spot, spot, back_sems, 8 + 4 * h + peer, 8 + 4 * h + peer, device).wait()
    spot = out_ref.at[pl.ds(own, half)]
    copy(spot, spot, back_sems, 16, 16, partner).start()
    spot = out_ref.at[pl.ds(other * half, half)]
    copy(spot, spot, back_sems, 16, 16, partner).wait()


def reduced_products(fields, neutral_row):
    vm = pl.BlockSpec(memory_space=pltpu.VMEM)
    half = TILES // 2

    def tiles(*lead):
        return pltpu.VMEM((*lead, 8, 128), jnp.float32)

    return pl.pallas_call(
        reduce_kernel,
        out_shape=jax.ShapeDtypeStruct((TILES, 8, 128), jnp.float32),
        in_specs=[vm, vm], out_specs=vm,
        scratch_shapes=[
            tiles(TILES), tiles(half), tiles(half), tiles(2, 4, half // 8), tiles(2, half // 8),
            tiles(2, 4, CHUNK), tiles(2, CHUNK), tiles(8, 2, CHUNK),
            pltpu.SemaphoreType.DMA((2, 1)), pltpu.SemaphoreType.DMA((2, 8)), pltpu.SemaphoreType.DMA((2, 8)),
            pltpu.SemaphoreType.DMA((2, 8)), pltpu.SemaphoreType.DMA((2, 17)),
        ],
        compiler_params=pltpu.CompilerParams(collective_id=1, has_side_effects=True,
                                             vmem_limit_bytes=40 * 1024 * 1024),
    )(fields, neutral_row)


def padded(value, sides, width):
    for axis, dim in sides:
        peers, length = (lax.axis_size(axis), value.shape[dim])
        up = [(i, (i + 1) % peers) for i in range(peers - 1)]
        down = [(j, i) for i, j in up]
        last = lax.slice_in_dim(value, length - width, length, axis=dim)
        first = lax.slice_in_dim(value, 0, width, axis=dim)
        before = lax.ppermute(last, axis, up)
        after = lax.ppermute(first, axis, down)
        value = jnp.concatenate([before, value, after], axis=dim)
    return value


def shift_depth(values, upward):
    padding = jnp.zeros_like(values[:, :, :1])
    if upward:
        return jnp.concatenate([padding, values[:, :, :-1]], axis=2)
    return jnp.concatenate([values[:, :, 1:], padding], axis=2)


def adjoint_apply(field_padded, coef_padded, margin):
    extent_x = field_padded.shape[0] - 2
    extent_y = field_padded.shape[1] - 2
    offset = 2 - margin

    def coef_at(component, step_x, step_y):
        return coef_padded[
            component,
            offset + step_x : offset + step_x + extent_x,
            offset + step_y : offset + step_y + extent_y,
            :,
        ][..., None]

    def field_at(step_x, step_y):
        return field_padded[1 + step_x : 1 + step_x + extent_x, 1 + step_y : 1 + step_y + extent_y]

    middle = field_at(0, 0)
    result = coef_at(0, 0, 0) * middle
    result = result + coef_at(1, -1, 0) * field_at(-1, 0)
    result = result + coef_at(2, 1, 0) * field_at(1, 0)
    result = result + coef_at(3, 0, -1) * field_at(0, -1)
    result = result + coef_at(4, 0, 1) * field_at(0, 1)
    result = result + shift_depth(coef_at(5, 0, 0) * middle, True)
    result = result + shift_depth(coef_at(6, 0, 0) * middle, False)
    return result


def face_rim(values):
    return padded(values, (("gx", 0), ("gy", 1)), 1)


def shards(adjoint_fields, center_coef, neighbor_coef, neutral):
    cells_x, cells_y, depth_cells, columns = adjoint_fields.shape
    stacked = jnp.concatenate([center_coef[:, None], neighbor_coef], axis=1)
    coef_padded = padded(stacked, (("gx", 2), ("gy", 3)), 2)
    adjoint_now = adjoint_fields
    for stepper in range(center_coef.shape[0] - 1, 0, -1):
        late_coef = coef_padded[stepper]
        early_coef = coef_padded[stepper - 1]
        slope_late = adjoint_apply(face_rim(adjoint_now), late_coef, 0)
        trial_field = adjoint_now + STEP_SIZE * slope_late
        slope_early = adjoint_apply(face_rim(trial_field), early_coef, 0)
        adjoint_now = adjoint_now + 0.5 * STEP_SIZE * (slope_late + slope_early)
    cell_count = cells_x * lax.axis_size("gx") * cells_y * lax.axis_size("gy") * depth_cells
    flattened = adjoint_now.reshape(-1, columns)
    packed = reduced_products(flattened, neutral.reshape(1, -1))
    orthonormal, factor = orthonormalize(packed, flattened, neutral.reshape(-1, 1), cell_count)
    orthonormal = orthonormal.reshape(adjoint_now.shape)
    return (orthonormal, factor)


def solution(mesh):
    in_specs = (
        P("gx", "gy", None, None),
        P(None, "gx", "gy", None),
        P(None, None, "gx", "gy", None),
        P("gx", "gy", None),
    )
    out_specs = (P("gx", "gy", None, None), P())
    return jax.shard_map(shards, mesh=mesh, in_specs=in_specs, out_specs=out_specs, check_vma=False)
```

```python
import functools

import jax
import jax.numpy as jnp
from jax import lax
from jax.experimental import pallas as pl
from jax.experimental.pallas import tpu as pltpu
from jax.sharding import PartitionSpec as P

STEP_SIZE = 0.15
EPSILON = 1e-06
HIGHEST = lax.Precision.HIGHEST


def dot_nt(a, b):
    return lax.dot_general(a, b, (((1,), (1,)), ((), ())), precision=HIGHEST,
                           preferred_element_type=jnp.float32)


def block_index(i, j):
    return i * (i + 1) // 2 + j


def lanes(value, column):
    return jnp.broadcast_to(value[:, column:column + 1], (8, 128))


def rows(value, row):
    return jnp.broadcast_to(value[row:row + 1, :], (8, 128))


def factor_diagonal(block_ref, upper_ref, inverse_ref):
    sub = lax.broadcasted_iota(jnp.int32, (8, 128), 0)
    lane = lax.broadcasted_iota(jnp.int32, (8, 128), 1)
    left = [block_ref[8 * i:8 * i + 8, :] for i in range(16)]
    right = [jnp.where(lane == sub + 8 * i, 1.0, 0.0).astype(jnp.float32) for i in range(16)]
    for k in range(16):
        base = 8 * k
        columns = [lanes(left[k], base + r) for r in range(8)]
        entry = {(q, r): rows(columns[r], q) for r in range(8) for q in range(r, 8)}
        u = [rows(left[k], r) for r in range(8)]
        v = [rows(right[k], r) for r in range(8)]
        scale = []
        lower = {}
        for r in range(8):
            s = lax.rsqrt(entry[r, r])
            scale.append(s)
            for q in range(r + 1, 8):
                lower[q, r] = entry[q, r] * s
            for q in range(r + 1, 8):
                for t in range(r + 1, q + 1):
                    entry[q, t] = entry[q, t] - lower[q, r] * lower[t, r]
            u[r] = u[r] * s
            v[r] = v[r] * s
            for q in range(r + 1, 8):
                u[q] = u[q] - lower[q, r] * u[r]
                v[q] = v[q] - lower[q, r] * v[r]
        for i in range(k + 1, 16):
            col = [lanes(left[i], base + r) for r in range(8)]
            for r in range(8):
                col[r] = col[r] * scale[r]
                for q in range(r + 1, 8):
                    col[q] = col[q] - lower[q, r] * col[r]
            for r in range(8):
                left[i] = left[i] - col[r] * u[r]
                right[i] = right[i] - col[r] * v[r]
        up = u[0]
        inv = v[0]
        for r in range(1, 8):
            up = jnp.where(sub == r, u[r], up)
            inv = jnp.where(sub == r, v[r], inv)
        upper_ref[base:base + 8, :] = jnp.where(lane >= sub + base, up, 0.0)
        inverse_ref[base:base + 8, :] = inv


def orthonormalize_kernel(cells, packed_ref, fields_ref, neutral_ref, out_ref, factor_ref,
                          gram, work, block, upper, inverse):
    nb = 4
    squared = packed_ref[0, 80, 1:2, :]
    aligned = [packed_ref[j // 2, 80 + j % 2, 0:1, :] for j in range(nb)]
    weight = [a / (squared + EPSILON) for a in aligned]
    ratio = jnp.sqrt(squared + 2 * EPSILON) / (squared + EPSILON)
    removed = [a * ratio for a in aligned]
    for i in range(nb):
        tall = jnp.broadcast_to(removed[i], (128, 128)).T
        for j in range(i + 1):
            b = block_index(i, j)
            raw = packed_ref[:, 8 * b:8 * b + 8].reshape(128, 128)
            gram[128 * i:128 * i + 128, 128 * j:128 * j + 128] = (raw - tall * removed[j]) * (1.0 / cells)
    for j in range(nb):
        work[:, 128 * j:128 * j + 128] = fields_ref[:, 128 * j:128 * j + 128] - neutral_ref[...] * weight[j]
    for j in range(nb):
        here = pl.ds(128 * j, 128)
        block[...] = gram[here, here]
        factor_diagonal(block, upper, inverse)
        factor_ref[here, here] = upper[...].T
        inv = inverse[...]
        panels = {}
        for i in range(j + 1, nb):
            panels[i] = dot_nt(gram[128 * i:128 * i + 128, here], inv)
            factor_ref[128 * i:128 * i + 128, here] = panels[i]
            factor_ref[here, 128 * i:128 * i + 128] = jnp.zeros((128, 128), jnp.float32)
        q = dot_nt(work[:, here], inv)
        out_ref[:, here] = q
        for i in range(j + 1, nb):
            for k in range(j + 1, i + 1):
                there = pl.ds(128 * k, 128)
                gram[128 * i:128 * i + 128, there] = gram[128 * i:128 * i + 128, there] - dot_nt(panels[i], panels[k])
        for k in range(j + 1, nb):
            there = pl.ds(128 * k, 128)
            work[:, there] = work[:, there] - dot_nt(q, panels[k])


def orthonormalize(packed, fields, neutral_column, cells):
    n = fields.shape[0]
    vm = pl.BlockSpec(memory_space=pltpu.VMEM)
    return pl.pallas_call(
        functools.partial(orthonormalize_kernel, cells),
        out_shape=(jax.ShapeDtypeStruct((n, 512), jnp.float32), jax.ShapeDtypeStruct((512, 512), jnp.float32)),
        in_specs=[vm] * 3, out_specs=(vm, vm),
        scratch_shapes=[pltpu.VMEM((512, 512), jnp.float32), pltpu.VMEM((n, 512), jnp.float32),
                        pltpu.VMEM((128, 128), jnp.float32), pltpu.VMEM((128, 128), jnp.float32),
                        pltpu.VMEM((128, 128), jnp.float32)],
        compiler_params=pltpu.CompilerParams(vmem_limit_bytes=40 * 1024 * 1024),
    )(packed, fields, neutral_column)


MESH = pl.DeviceIdType.MESH
TILES = 96
QUARTER = 48
PIECE = 12
CHUNK = 3
LEVEL_OF_ROUND = (2, 1, 1, 0)


def evolve_kernel(fields_ref, center_ref, neighbor_ref, neutral_ref, evolved_ref, out_ref,
                  coef, trial, late, slope, x_send, y_send, x_recv, y_recv,
                  pack, from_core, mid, from_first, low, from_second, tail, from_third,
                  x_sems, y_sems, core_sems, first_sems, second_sems, third_sems, back_sems):
    gx, gy = lax.axis_index("gx"), lax.axis_index("gy")
    core, y = lax.rem(gx, 2), lax.div(gx, 2)
    z, x = lax.rem(gy, 8), lax.div(gy, 8)
    other = 1 - core
    partner = (gx + 1 - 2 * core, gy)
    x_sides = ((lax.rem(gx + 1, 8), gy), (lax.rem(gx + 7, 8), gy))
    y_sides = ((gx, lax.rem(gy + 1, 32)), (gx, lax.rem(gy + 31, 32)))

    def along_y(step):
        peer = lax.rem(y + step, 4)
        return peer, (2 * peer + core, gy)

    def along_x(step):
        peer = lax.rem(x + step, 4)
        return peer, (gx, 8 * peer + z)

    def along_z(step):
        peer = lax.rem(z + step, 8)
        return peer, (gx, 8 * x + peer)

    barrier = pltpu.get_barrier_semaphore()
    greeted = [*x_sides, *y_sides, partner]
    greeted += [along_y(step)[1] for step in range(1, 4)] + [along_x(step)[1] for step in range(1, 4)]
    greeted += [along_z(step)[1] for step in range(1, 8)]
    for device in greeted:
        pl.semaphore_signal(barrier, inc=1, device_id=device, device_id_type=MESH)

    def spread(level):
        depth = lax.broadcasted_iota(jnp.int32, (16, 128), 0)
        for component in range(7):
            if component == 0:
                table = center_ref[32 * level:32 * level + 32, :].T
            else:
                start = 192 * level + 32 * (component - 1)
                table = neighbor_ref[start:start + 32, :].T
            for cell in range(32):
                value = jnp.broadcast_to(table[:, cell:cell + 1], (16, 128))
                if component == 5:
                    value = jnp.where(depth == 15, 0.0, value)
                if component == 6:
                    value = jnp.where(depth == 0, 0.0, value)
                coef[level, component, cell // 8, cell % 8] = value

    def lanes_of(g):
        return slice(128 * g, 128 * g + 128)

    def held(r, g, i):
        if r == 0:
            return fields_ref[i, :, :, lanes_of(g)]
        if r == 2:
            return evolved_ref[128 * i:128 * i + 128, lanes_of(g)].reshape(8, 16, 128)
        return trial[g, i]

    def face_copies(r, g):
        copies = []
        for side in range(2):
            copies.append(pltpu.make_async_remote_copy(
                src_ref=x_send.at[r, g, side], dst_ref=x_recv.at[r, g, side],
                send_sem=x_sems.at[0, r, g, side], recv_sem=x_sems.at[1, r, g, side],
                device_id=x_sides[side], device_id_type=MESH))
            copies.append(pltpu.make_async_remote_copy(
                src_ref=y_send.at[r, g, side], dst_ref=y_recv.at[r, g, side],
                send_sem=y_sems.at[0, r, g, side], recv_sem=y_sems.at[1, r, g, side],
                device_id=y_sides[side], device_id_type=MESH))
        return copies

    def send_faces(r, g):
        level = LEVEL_OF_ROUND[r]
        copies = face_copies(r, g)
        x_edge = (gx < 7, gx > 0)
        y_edge = (gy < 31, gy > 0)
        for side in range(2):
            i = (3, 0)[side]
            x_send[r, g, side] = jnp.where(x_edge[side], coef[level, 1 + side, i] * held(r, g, i), 0.0)
            copies[2 * side].start()
        for side in range(2):
            j = (7, 0)[side]
            for i in range(4):
                value = held(r, g, i)[j]
                y_send[r, g, side, i] = jnp.where(y_edge[side], coef[level, 3 + side, i, j] * value, 0.0)
            copies[2 * side + 1].start()

    def local_terms(r, g):
        level = LEVEL_OF_ROUND[r]
        for i in range(4):
            v = held(r, g, i)
            total = coef[level, 0, i] * v
            up = (coef[level, 5, i] * v).reshape(128, 128)
            down = (coef[level, 6, i] * v).reshape(128, 128)
            total = total + pltpu.roll(up, 1, 0).reshape(8, 16, 128)
            total = total + pltpu.roll(down, 127, 0).reshape(8, 16, 128)
            if i > 0:
                total = total + coef[level, 1, i - 1] * held(r, g, i - 1)
            if i < 3:
                total = total + coef[level, 2, i + 1] * held(r, g, i + 1)
            zero = jnp.zeros((1, 16, 128), jnp.float32)
            total = total + jnp.concatenate([zero, (coef[level, 3, i] * v)[:7]], axis=0)
            total = total + jnp.concatenate([(coef[level, 4, i] * v)[1:], zero], axis=0)
            slope[g, i] = total

    def finish(r, g):
        for c in face_copies(r, g):
            c.wait()
        for i in range(4):
            total = slope[g, i]
            if i == 0:
                total = total + x_recv[r, g, 0]
            if i == 3:
                total = total + x_recv[r, g, 1]
            total = jnp.concatenate([(total[0] + y_recv[r, g, 0, i])[None], total[1:7],
                                     (total[7] + y_recv[r, g, 1, i])[None]], axis=0)
            start = held(0 if r < 2 else 2, g, i)
            if r % 2 == 0:
                late[g, i] = total
                trial[g, i] = start + STEP_SIZE * total
            else:
                done = start + 0.5 * STEP_SIZE * (late[g, i] + total)
                evolved_ref[128 * i:128 * i + 128, lanes_of(g)] = done.reshape(128, 128)

    def copy(src, dst, sems, mine, theirs, device):
        return pltpu.make_async_remote_copy(src_ref=src, dst_ref=dst, send_sem=sems.at[0, theirs],
                                            recv_sem=sems.at[1, mine], device_id=device, device_id_type=MESH)

    def core_copy(b):
        span = pl.ds(8 * b, 8) if b < 10 else pl.ds(80, 2)
        return copy(pack.at[other, span], from_core.at[span], core_sems, b, b, partner)

    def first_start(h):
        me, along = ((y, along_y), (x, along_x))[h]
        for step in range(1, 4):
            peer, device = along(step)
            copy(mid.at[pl.ds(h * QUARTER + peer * PIECE, PIECE)], from_first.at[h, me], first_sems,
                 4 * h + me, 4 * h + peer, device).start()

    spread(2)
    pl.semaphore_wait(barrier, len(greeted))
    for r in range(4):
        for g in range(4):
            if r > 0:
                finish(r - 1, g)
            send_faces(r, g)
            local_terms(r, g)
        if r < 2:
            spread(1 - r)

    sub = lax.broadcasted_iota(jnp.int32, (8, 512), 0)
    row = neutral_ref[...]
    first_row = jnp.where(sub == 0, row, 0.0)
    squared = jnp.sum(row * row)
    for g in range(4):
        finish(3, g)
        mine = evolved_ref[:, lanes_of(g)]
        for j in range(g + 1):
            b = g * (g + 1) // 2 + j
            product = lax.dot_general(mine, evolved_ref[:, lanes_of(j)], (((0,), (0,)), ((), ())),
                                      precision=HIGHEST, preferred_element_type=jnp.float32)
            pack[:, 8 * b:8 * b + 8] = product.reshape(2, 8, 8, 128)
            core_copy(b).start()
        aligned = lax.dot_general(first_row, mine, (((1,), (0,)), ((), ())), precision=HIGHEST,
                                  preferred_element_type=jnp.float32)
        pack[g // 2, 80 + g % 2] = jnp.where(sub[:, :128] == 1, squared, aligned)
        if g == 2:
            for b in range(6):
                core_copy(b).wait()
            mid[0:QUARTER] = pack[core, 0:QUARTER] + from_core[0:QUARTER]
            first_start(0)
    core_copy(10).start()
    for b in range(6, 11):
        core_copy(b).wait()
    mid[QUARTER:82] = pack[core, QUARTER:82] + from_core[QUARTER:82]
    mid[82:TILES] = jnp.zeros((TILES - 82, 8, 128), jnp.float32)
    first_start(1)

    for h in range(2):
        me, along = ((y, along_y), (x, along_x))[h]
        total = mid[pl.ds(h * QUARTER + me * PIECE, PIECE)]
        for step in range(1, 4):
            peer, device = along(step)
            copy(mid.at[pl.ds(h * QUARTER + peer * PIECE, PIECE)], from_first.at[h, peer], first_sems,
                 4 * h + peer, 4 * h + peer, device).wait()
            total = total + from_first[h, peer]
        low[h] = total
        me, along = ((x, along_x), (y, along_y))[h]
        for step in range(1, 4):
            peer, device = along(step)
            copy(low.at[h, pl.ds(peer * CHUNK, CHUNK)], from_second.at[h, me], second_sems,
                 4 * h + me, 4 * h + peer, device).start()
    for h in range(2):
        me, along = ((x, along_x), (y, along_y))[h]
        total = low[h, pl.ds(me * CHUNK, CHUNK)]
        for step in range(1, 4):
            peer, device = along(step)
            copy(low.at[h, pl.ds(peer * CHUNK, CHUNK)], from_second.at[h, peer], second_sems,
                 4 * h + peer, 4 * h + peer, device).wait()
            total = total + from_second[h, peer]
        tail[h] = total
    for step in range(1, 8):
        peer, device = along_z(step)
        copy(tail, from_third.at[z], third_sems, z, peer, device).start()
    from_third[z] = tail[...]
    for step in range(1, 8):
        peer, device = along_z(step)
        copy(tail, from_third.at[peer], third_sems, peer, peer, device).wait()
    final = from_third[0]
    for p in range(1, 8):
        final = final + from_third[p]

    places = (y * PIECE + x * CHUNK, QUARTER + x * PIECE + y * CHUNK)
    for h in range(2):
        out_ref[core, pl.ds(places[h], CHUNK)] = final[h]
    for h in range(2):
        me, along = ((x, along_x), (y, along_y))[h]
        for step in range(1, 4):
            peer, device = along(step)
            spot = out_ref.at[core, pl.ds(places[h], CHUNK)]
            copy(spot, spot, back_sems, 4 * h + me, 4 * h + peer, device).start()
    for h in range(2):
        me, along = ((x, along_x), (y, along_y))[h]
        outer, along_outer = ((y, along_y), (x, along_x))[h]
        for step in range(1, 4):
            peer, device = along(step)
            spot = out_ref.at[core, pl.ds(h * QUARTER + outer * PIECE + peer * CHUNK, CHUNK)]
            copy(spot, spot, back_sems, 4 * h + peer, 4 * h + peer, device).wait()
        for step in range(1, 4):
            peer, device = along_outer(step)
            spot = out_ref.at[core, pl.ds(h * QUARTER + outer * PIECE, PIECE)]
            copy(spot, spot, back_sems, 8 + 4 * h + outer, 8 + 4 * h + peer, device).start()

    def forward(h, owner):
        spot = out_ref.at[core, pl.ds(h * QUARTER + owner * PIECE, PIECE)]
        return copy(spot, spot, back_sems, 16 + 4 * h + owner, 16 + 4 * h + owner, partner)

    for h in range(2):
        forward(h, (y, x)[h]).start()
    for step in range(1, 4):
        for h in range(2):
            peer, device = (along_y, along_x)[h](step)
            spot = out_ref.at[core, pl.ds(h * QUARTER + peer * PIECE, PIECE)]
            copy(spot, spot, back_sems, 8 + 4 * h + peer, 8 + 4 * h + peer, device).wait()
            forward(h, peer).start()
    for h in range(2):
        for owner in range(4):
            spot = out_ref.at[other, pl.ds(h * QUARTER + owner * PIECE, PIECE)]
            copy(spot, spot, back_sems, 16 + 4 * h + owner, 16 + 4 * h + owner, partner).wait()


def evolve_and_reduce(fields, center, neighbor, neutral_row):
    vm = pl.BlockSpec(memory_space=pltpu.VMEM)

    def tiles(*lead):
        return pltpu.VMEM((*lead, 8, 128), jnp.float32)

    def columns(*lead):
        return pltpu.VMEM((*lead, 16, 128), jnp.float32)

    return pl.pallas_call(
        evolve_kernel,
        out_shape=(jax.ShapeDtypeStruct((512, 512), jnp.float32),
                   jax.ShapeDtypeStruct((2, TILES, 8, 128), jnp.float32)),
        in_specs=[vm] * 4, out_specs=(vm, vm),
        scratch_shapes=[
            columns(3, 7, 4, 8), columns(4, 4, 8), columns(4, 4, 8), columns(4, 4, 8),
            columns(4, 4, 2, 8), columns(4, 4, 2, 4), columns(4, 4, 2, 8), columns(4, 4, 2, 4),
            tiles(2, TILES), tiles(TILES), tiles(TILES), tiles(2, 4, PIECE), tiles(2, PIECE),
            tiles(2, 4, CHUNK), tiles(2, CHUNK), tiles(8, 2, CHUNK),
            pltpu.SemaphoreType.DMA((2, 4, 4, 2)), pltpu.SemaphoreType.DMA((2, 4, 4, 2)),
            pltpu.SemaphoreType.DMA((2, 11)), pltpu.SemaphoreType.DMA((2, 8)), pltpu.SemaphoreType.DMA((2, 8)),
            pltpu.SemaphoreType.DMA((2, 8)), pltpu.SemaphoreType.DMA((2, 24)),
        ],
        compiler_params=pltpu.CompilerParams(collective_id=1, has_side_effects=True,
                                             vmem_limit_bytes=48 * 1024 * 1024),
    )(fields, center, neighbor, neutral_row)


def shards(adjoint_fields, center_coef, neighbor_coef, neutral):
    cells_x, cells_y, depth_cells, columns = adjoint_fields.shape
    cell_count = cells_x * lax.axis_size("gx") * cells_y * lax.axis_size("gy") * depth_cells
    evolved, packed = evolve_and_reduce(
        adjoint_fields, center_coef.reshape(-1, depth_cells), neighbor_coef.reshape(-1, depth_cells),
        neutral.reshape(1, -1))
    orthonormal, factor = orthonormalize(packed, evolved, neutral.reshape(-1, 1), cell_count)
    return (orthonormal.reshape(adjoint_fields.shape), factor)


def solution(mesh):
    in_specs = (
        P("gx", "gy", None, None),
        P(None, "gx", "gy", None),
        P(None, None, "gx", "gy", None),
        P("gx", "gy", None),
    )
    out_specs = (P("gx", "gy", None, None), P())
    return jax.shard_map(shards, mesh=mesh, in_specs=in_specs, out_specs=out_specs, check_vma=False)
```

```python
import functools

import jax
import jax.numpy as jnp
from jax import lax
from jax.experimental import pallas as pl
from jax.experimental.pallas import tpu as pltpu
from jax.sharding import PartitionSpec as P

STEP_SIZE = 0.15
EPSILON = 1e-06
HIGHEST = lax.Precision.HIGHEST


def dot_nt(a, b):
    return lax.dot_general(a, b, (((1,), (1,)), ((), ())), precision=HIGHEST,
                           preferred_element_type=jnp.float32)


def lanes(value, column):
    return jnp.broadcast_to(value[:, column:column + 1], (8, 128))


def rows(value, row):
    return jnp.broadcast_to(value[row:row + 1, :], (8, 128))


def factor_diagonal(block_ref, upper_ref, inverse_ref, aside):
    sub = lax.broadcasted_iota(jnp.int32, (8, 128), 0)
    lane = lax.broadcasted_iota(jnp.int32, (8, 128), 1)
    left = [block_ref[8 * i:8 * i + 8, :] for i in range(16)]
    right = [jnp.where(lane == sub + 8 * i, 1.0, 0.0).astype(jnp.float32) for i in range(16)]
    for k in range(16):
        base = 8 * k
        columns = [lanes(left[k], base + r) for r in range(8)]
        entry = {(q, r): rows(columns[r], q) for r in range(8) for q in range(r, 8)}
        u = [rows(left[k], r) for r in range(8)]
        v = [rows(right[k], r) for r in range(8)]
        scale = []
        lower = {}
        for r in range(8):
            s = lax.rsqrt(entry[r, r])
            scale.append(s)
            for q in range(r + 1, 8):
                lower[q, r] = entry[q, r] * s
            for q in range(r + 1, 8):
                for t in range(r + 1, q + 1):
                    entry[q, t] = entry[q, t] - lower[q, r] * lower[t, r]
            u[r] = u[r] * s
            v[r] = v[r] * s
            for q in range(r + 1, 8):
                u[q] = u[q] - lower[q, r] * u[r]
                v[q] = v[q] - lower[q, r] * v[r]
        for i in range(k + 1, 16):
            col = [lanes(left[i], base + r) for r in range(8)]
            for r in range(8):
                col[r] = col[r] * scale[r]
                for q in range(r + 1, 8):
                    col[q] = col[q] - lower[q, r] * col[r]
            for r in range(8):
                left[i] = left[i] - col[r] * u[r]
                right[i] = right[i] - col[r] * v[r]
        up = u[0]
        inv = v[0]
        for r in range(1, 8):
            up = jnp.where(sub == r, u[r], up)
            inv = jnp.where(sub == r, v[r], inv)
        upper_ref[base:base + 8, :] = jnp.where(lane >= sub + base, up, 0.0)
        inverse_ref[base:base + 8, :] = inv
        for work in aside[len(aside) * k // 16:len(aside) * (k + 1) // 16]:
            work()


def orthonormalize_kernel(cells, packed_ref, fields_ref, wide_ref, out_hbm, factor_hbm,
                          gram, work, out_ref, factor_ref, upper, inverse, sems):
    nb = 4
    squared = packed_ref[0, 80, 1:2, :]
    aligned = [packed_ref[j // 2, 80 + j % 2, 0:1, :] for j in range(nb)]
    weight = [a / (squared + EPSILON) for a in aligned]
    ratio = jnp.sqrt(squared + 2 * EPSILON) / (squared + EPSILON)
    removed = [a * ratio for a in aligned]

    def span(j):
        return slice(128 * j, 128 * j + 128)

    def prepare(i, j):
        b = i * (i + 1) // 2 + j
        tall = jnp.broadcast_to(removed[i], (128, 128)).T
        raw = packed_ref[:, 8 * b:8 * b + 8].reshape(128, 128)
        gram[span(i), span(j)] = (raw - tall * removed[j]) * (1.0 / cells)
        if i != j:
            factor_ref[span(j), span(i)] = jnp.zeros((128, 128), jnp.float32)

    def project(i, j):
        work[span(i), span(j)] = fields_ref[span(i), span(j)] - wide_ref[span(i)] * weight[j]

    def panel(i, j):
        factor_ref[span(i), span(j)] = dot_nt(gram[span(i), span(j)], inverse[j])

    def update(i, k, j):
        gram[span(i), span(k)] = gram[span(i), span(k)] - dot_nt(factor_ref[span(i), span(j)],
                                                                factor_ref[span(k), span(j)])

    def result(c, j):
        out_ref[span(c), span(j)] = dot_nt(work[span(c), span(j)], inverse[j])

    def remove(c, k, j):
        work[span(c), span(k)] = work[span(c), span(k)] - dot_nt(out_ref[span(c), span(j)],
                                                                factor_ref[span(k), span(j)])

    def sent(j):
        here = pl.ds(128 * j, 128)
        return pltpu.make_async_copy(out_ref.at[:, here], out_hbm.at[:, here], sems.at[j])

    factor_copy = pltpu.make_async_copy(factor_ref, factor_hbm, sems.at[nb])
    prepare(0, 0)
    aside = [functools.partial(prepare, i, j) for i in range(1, nb) for j in range(i + 1)]
    aside += [functools.partial(project, i, j) for j in range(nb) for i in range(nb)]
    for j in range(nb):
        factor_diagonal(gram.at[span(j), span(j)], upper, inverse.at[j], aside)
        factor_ref[span(j), span(j)] = upper[...].T
        aside = []
        if j + 1 < nb:
            panel(j + 1, j)
            update(j + 1, j + 1, j)
            aside += [functools.partial(panel, i, j) for i in range(j + 2, nb)]
            aside += [functools.partial(update, i, k, j) for i in range(j + 2, nb) for k in range(j + 1, i + 1)]
            aside += [functools.partial(result, c, j) for c in range(nb)]
            aside += [sent(j).start]
            aside += [functools.partial(remove, c, k, j) for k in range(j + 1, nb) for c in range(nb)]
    factor_copy.start()
    for c in range(nb):
        result(c, nb - 1)
    sent(nb - 1).start()
    for j in range(nb):
        sent(j).wait()
    factor_copy.wait()


def orthonormalize(packed, fields, wide, cells):
    n = fields.shape[0]
    vm = pl.BlockSpec(memory_space=pltpu.VMEM)
    hbm = pl.BlockSpec(memory_space=pltpu.HBM)
    return pl.pallas_call(
        functools.partial(orthonormalize_kernel, cells),
        out_shape=(jax.ShapeDtypeStruct((n, 512), jnp.float32), jax.ShapeDtypeStruct((512, 512), jnp.float32)),
        in_specs=[vm] * 3, out_specs=(hbm, hbm),
        scratch_shapes=[pltpu.VMEM((512, 512), jnp.float32), pltpu.VMEM((n, 512), jnp.float32),
                        pltpu.VMEM((n, 512), jnp.float32), pltpu.VMEM((512, 512), jnp.float32),
                        pltpu.VMEM((128, 128), jnp.float32), pltpu.VMEM((4, 128, 128), jnp.float32),
                        pltpu.SemaphoreType.DMA((5,))],
        compiler_params=pltpu.CompilerParams(vmem_limit_bytes=40 * 1024 * 1024),
    )(packed, fields, wide)


MESH = pl.DeviceIdType.MESH
TILES = 96
HALF = 48
PIECE = 6
LEVEL_OF_ROUND = (2, 1, 1, 0)


def evolve_kernel(fields_hbm, center_hbm, neighbor_hbm, neutral_hbm, evolved_ref, out_ref, wide_ref,
                  fields_ref, center_ref, neighbor_ref, neutral_ref,
                  coef, trial, late, slope, x_send, y_send, x_recv, y_recv,
                  pack, from_core, mid, from_plane, tail, from_ring,
                  in_sems, x_sems, y_sems, core_sems, plane_sems, ring_sems, back_sems):
    gx, gy = lax.axis_index("gx"), lax.axis_index("gy")
    core, y = lax.rem(gx, 2), lax.div(gx, 2)
    z, x = lax.rem(gy, 8), lax.div(gy, 8)
    other = 1 - core
    partner = (gx + 1 - 2 * core, gy)
    x_sides = ((lax.rem(gx + 1, 8), gy), (lax.rem(gx + 7, 8), gy))
    y_sides = ((gx, lax.rem(gy + 1, 32)), (gx, lax.rem(gy + 31, 32)))

    def on_plane(offset):
        peer_y, peer_x = lax.rem(y + offset[0], 4), lax.rem(x + offset[1], 4)
        return place_of(peer_y, peer_x), (2 * peer_y + core, 8 * peer_x + z)

    def place_of(at_y, at_x):
        return 8 * lax.rem(at_y + at_x, 2) + 2 * at_y + lax.div(at_x, 2)

    offsets = sorted(((a, b) for a in range(4) for b in range(4) if a or b),
                     key=lambda o: -(min(o[0], 4 - o[0]) + min(o[1], 4 - o[1])))
    place = place_of(y, x)

    def along_z(step):
        peer = lax.rem(z + step, 8)
        return peer, (gx, 8 * x + peer)

    barrier = pltpu.get_barrier_semaphore()
    greeted = [*x_sides, *y_sides, partner]
    greeted += [on_plane(offset)[1] for offset in offsets]
    greeted += [along_z(step)[1] for step in range(1, 8)]
    for device in greeted:
        pl.semaphore_signal(barrier, inc=1, device_id=device, device_id_type=MESH)
    loads = [pltpu.make_async_copy(neighbor_hbm, neighbor_ref, in_sems.at[0]),
             pltpu.make_async_copy(center_hbm, center_ref, in_sems.at[1])]
    for g in range(4):
        lanes = pl.ds(128 * g, 128)
        loads.append(pltpu.make_async_copy(fields_hbm.at[:, :, :, lanes], fields_ref.at[:, :, :, lanes],
                                           in_sems.at[2 + g]))
    loads.append(pltpu.make_async_copy(neutral_hbm, neutral_ref, in_sems.at[6]))
    for load in loads:
        load.start()

    def spread(level):
        depth = lax.broadcasted_iota(jnp.int32, (16, 128), 0)
        for component in range(7):
            if component == 0:
                table = center_ref[32 * level:32 * level + 32, :].T
            else:
                start = 192 * level + 32 * (component - 1)
                table = neighbor_ref[start:start + 32, :].T
            for cell in range(32):
                value = jnp.broadcast_to(table[:, cell:cell + 1], (16, 128))
                if component == 5:
                    value = jnp.where(depth == 15, 0.0, value)
                if component == 6:
                    value = jnp.where(depth == 0, 0.0, value)
                coef[level, component, cell // 8, cell % 8] = value

    def lanes_of(g):
        return slice(128 * g, 128 * g + 128)

    def held(r, g, i):
        if r == 0:
            return fields_ref[i, :, :, lanes_of(g)]
        if r == 2:
            return evolved_ref[128 * i:128 * i + 128, lanes_of(g)].reshape(8, 16, 128)
        return trial[g, i]

    def face_copies(r, g):
        copies = []
        for side in range(2):
            copies.append(pltpu.make_async_remote_copy(
                src_ref=x_send.at[r, g, side], dst_ref=x_recv.at[r, g, side],
                send_sem=x_sems.at[0, r, g, side], recv_sem=x_sems.at[1, r, g, side],
                device_id=x_sides[side], device_id_type=MESH))
            copies.append(pltpu.make_async_remote_copy(
                src_ref=y_send.at[r, g, side], dst_ref=y_recv.at[r, g, side],
                send_sem=y_sems.at[0, r, g, side], recv_sem=y_sems.at[1, r, g, side],
                device_id=y_sides[side], device_id_type=MESH))
        return copies

    def send_faces(r, g):
        level = LEVEL_OF_ROUND[r]
        copies = face_copies(r, g)
        x_edge = (gx < 7, gx > 0)
        y_edge = (gy < 31, gy > 0)
        for side in range(2):
            i = (3, 0)[side]
            x_send[r, g, side] = jnp.where(x_edge[side], coef[level, 1 + side, i] * held(r, g, i), 0.0)
            copies[2 * side].start()
        for side in range(2):
            j = (7, 0)[side]
            for i in range(4):
                value = held(r, g, i)[j]
                y_send[r, g, side, i] = jnp.where(y_edge[side], coef[level, 3 + side, i, j] * value, 0.0)
            copies[2 * side + 1].start()

    def local_terms(r, g):
        level = LEVEL_OF_ROUND[r]
        for i in range(4):
            v = held(r, g, i)
            total = coef[level, 0, i] * v
            up = (coef[level, 5, i] * v).reshape(128, 128)
            down = (coef[level, 6, i] * v).reshape(128, 128)
            total = total + pltpu.roll(up, 1, 0).reshape(8, 16, 128)
            total = total + pltpu.roll(down, 127, 0).reshape(8, 16, 128)
            if i > 0:
                total = total + coef[level, 1, i - 1] * held(r, g, i - 1)
            if i < 3:
                total = total + coef[level, 2, i + 1] * held(r, g, i + 1)
            zero = jnp.zeros((1, 16, 128), jnp.float32)
            total = total + jnp.concatenate([zero, (coef[level, 3, i] * v)[:7]], axis=0)
            total = total + jnp.concatenate([(coef[level, 4, i] * v)[1:], zero], axis=0)
            slope[g, i] = total

    def finish(r, g):
        parts = []
        for c in face_copies(r, g):
            c.wait()
        for i in range(4):
            total = slope[g, i]
            if i == 0:
                total = total + x_recv[r, g, 0]
            if i == 3:
                total = total + x_recv[r, g, 1]
            total = jnp.concatenate([(total[0] + y_recv[r, g, 0, i])[None], total[1:7],
                                     (total[7] + y_recv[r, g, 1, i])[None]], axis=0)
            start = held(0 if r < 2 else 2, g, i)
            if r % 2 == 0:
                late[g, i] = total
                trial[g, i] = start + STEP_SIZE * total
            else:
                done = start + 0.5 * STEP_SIZE * (late[g, i] + total)
                evolved_ref[128 * i:128 * i + 128, lanes_of(g)] = done.reshape(128, 128)
                if r == 3:
                    parts.append(jnp.sum(done.reshape(16, 8, 128) * wide_ref[128 * i:128 * i + 128].reshape(16, 8, 128),
                                         axis=0))
        return parts

    def copy(src, dst, sems, mine, theirs, device):
        return pltpu.make_async_remote_copy(src_ref=src, dst_ref=dst, send_sem=sems.at[0, theirs],
                                            recv_sem=sems.at[1, mine], device_id=device, device_id_type=MESH)

    def core_copy(b):
        span = pl.ds(8 * b, 8) if b < 10 else pl.ds(80, 2)
        return copy(pack.at[other, span], from_core.at[span], core_sems, b, b, partner)

    def plane_start(wave):
        for offset in offsets:
            peer, device = on_plane(offset)

            @pl.when(lax.div(peer, 8) == wave)
            def _():
                copy(mid.at[pl.ds(peer * PIECE, PIECE)], from_plane.at[place], plane_sems, place, peer,
                     device).start()

    loads[0].wait()
    loads[1].wait()
    spread(2)
    pl.semaphore_wait(barrier, len(greeted))
    for r in range(4):
        for g in range(4):
            if r > 0:
                finish(r - 1, g)
            else:
                loads[2 + g].wait()
            send_faces(r, g)
            local_terms(r, g)
        if r < 2:
            spread(1 - r)
        if r == 2:
            loads[6].wait()
            table = neutral_ref[...].T
            for cell in range(32):
                wide_ref[16 * cell:16 * cell + 16] = jnp.broadcast_to(table[:, cell:cell + 1], (16, 128))

    sub = lax.broadcasted_iota(jnp.int32, (8, 128), 0)
    squared = jnp.sum(neutral_ref[...] * neutral_ref[...])
    for g in range(4):
        parts = finish(3, g)
        product = lax.dot_general(evolved_ref[:, lanes_of(g)], evolved_ref[:, :128 * g + 128],
                                  (((0,), (0,)), ((), ())), precision=HIGHEST,
                                  preferred_element_type=jnp.float32)
        for j in range(g + 1):
            b = g * (g + 1) // 2 + j
            pack[:, 8 * b:8 * b + 8] = product[:, 128 * j:128 * j + 128].reshape(2, 8, 8, 128)
            core_copy(b).start()
        aligned = jnp.sum(parts[0] + parts[1] + (parts[2] + parts[3]), axis=0, keepdims=True)
        pack[g // 2, 80 + g % 2] = jnp.where(sub == 1, squared, aligned)
        if g == 2:
            for b in range(6):
                core_copy(b).wait()
            mid[0:HALF] = pack[core, 0:HALF] + from_core[0:HALF]
            plane_start(0)
    core_copy(10).start()
    for b in range(6, 11):
        core_copy(b).wait()
    mid[HALF:82] = pack[core, HALF:82] + from_core[HALF:82]
    mid[82:TILES] = jnp.zeros((TILES - 82, 8, 128), jnp.float32)
    plane_start(1)

    total = mid[pl.ds(place * PIECE, PIECE)]
    for offset in reversed(offsets):
        peer, device = on_plane(offset)
        copy(mid.at[pl.ds(peer * PIECE, PIECE)], from_plane.at[peer], plane_sems, peer, peer, device).wait()
        total = total + from_plane[peer]
    tail[...] = total
    for step in (4, 3, 5, 2, 6, 1, 7):
        peer, device = along_z(step)
        copy(tail, from_ring.at[z], ring_sems, z, peer, device).start()
    from_ring[z] = total
    for step in (1, 7, 2, 6, 3, 5, 4):
        peer, device = along_z(step)
        copy(tail, from_ring.at[peer], ring_sems, peer, peer, device).wait()
    final = from_ring[0]
    for p in range(1, 8):
        final = final + from_ring[p]

    def back(side, owner, device):
        spot = out_ref.at[side, pl.ds(owner * PIECE, PIECE)]
        return copy(spot, spot, back_sems, owner, owner, device)

    def forward(side, owner):
        spot = out_ref.at[side, pl.ds(owner * PIECE, PIECE)]
        return copy(spot, spot, back_sems, 16 + owner, 16 + owner, partner)

    out_ref[core, pl.ds(place * PIECE, PIECE)] = final
    for offset in offsets:
        peer, device = on_plane(offset)
        spot = out_ref.at[core, pl.ds(place * PIECE, PIECE)]
        copy(spot, spot, back_sems, place, peer, device).start()
    forward(core, place).start()
    for offset in reversed(offsets):
        peer, device = on_plane(offset)
        back(core, peer, device).wait()
        forward(core, peer).start()
    for owner in range(16):
        forward(other, owner).wait()


def evolve_and_reduce(fields, center, neighbor, neutral):
    vm = pl.BlockSpec(memory_space=pltpu.VMEM)
    hbm = pl.BlockSpec(memory_space=pltpu.HBM)

    def tiles(*lead):
        return pltpu.VMEM((*lead, 8, 128), jnp.float32)

    def columns(*lead):
        return pltpu.VMEM((*lead, 16, 128), jnp.float32)

    arguments = (fields, center, neighbor, neutral)
    return pl.pallas_call(
        evolve_kernel,
        out_shape=(jax.ShapeDtypeStruct((512, 512), jnp.float32),
                   jax.ShapeDtypeStruct((2, TILES, 8, 128), jnp.float32),
                   jax.ShapeDtypeStruct((512, 128), jnp.float32)),
        in_specs=[hbm] * 4, out_specs=(vm, vm, vm),
        scratch_shapes=[
            *[pltpu.VMEM(a.shape, jnp.float32) for a in arguments],
            columns(3, 7, 4, 8), columns(4, 4, 8), columns(4, 4, 8), columns(4, 4, 8),
            columns(4, 4, 2, 8), columns(4, 4, 2, 4), columns(4, 4, 2, 8), columns(4, 4, 2, 4),
            tiles(2, TILES), tiles(TILES), tiles(TILES), tiles(16, PIECE), tiles(PIECE), tiles(8, PIECE),
            pltpu.SemaphoreType.DMA((7,)),
            pltpu.SemaphoreType.DMA((2, 4, 4, 2)), pltpu.SemaphoreType.DMA((2, 4, 4, 2)),
            pltpu.SemaphoreType.DMA((2, 11)), pltpu.SemaphoreType.DMA((2, 16)),
            pltpu.SemaphoreType.DMA((2, 8)), pltpu.SemaphoreType.DMA((2, 32)),
        ],
        compiler_params=pltpu.CompilerParams(collective_id=1, has_side_effects=True,
                                             vmem_limit_bytes=48 * 1024 * 1024),
    )(*arguments)


def shards(adjoint_fields, center_coef, neighbor_coef, neutral):
    cells_x, cells_y, depth_cells, columns = adjoint_fields.shape
    cell_count = cells_x * lax.axis_size("gx") * cells_y * lax.axis_size("gy") * depth_cells
    evolved, packed, wide = evolve_and_reduce(
        adjoint_fields, center_coef.reshape(-1, depth_cells), neighbor_coef.reshape(-1, depth_cells),
        neutral.reshape(-1, depth_cells))
    orthonormal, factor = orthonormalize(packed, evolved, wide, cell_count)
    return (orthonormal.reshape(adjoint_fields.shape), factor)


def solution(mesh):
    in_specs = (
        P("gx", "gy", None, None),
        P(None, "gx", "gy", None),
        P(None, None, "gx", "gy", None),
        P("gx", "gy", None),
    )
    out_specs = (P("gx", "gy", None, None), P())
    return jax.shard_map(shards, mesh=mesh, in_specs=in_specs, out_specs=out_specs, check_vma=False)
```

```python
import functools

import jax
import jax.numpy as jnp
from jax import lax
from jax.experimental import pallas as pl
from jax.experimental.pallas import tpu as pltpu
from jax.sharding import PartitionSpec as P

STEP_SIZE = 0.15
EPSILON = 1e-06
HIGHEST = lax.Precision.HIGHEST


def dot_nt(a, b):
    return lax.dot_general(a, b, (((1,), (1,)), ((), ())), precision=HIGHEST,
                           preferred_element_type=jnp.float32)


def lanes(value, column):
    return jnp.broadcast_to(value[:, column:column + 1], (8, 128))


def rows(value, row):
    return jnp.broadcast_to(value[row:row + 1, :], (8, 128))


def three_parts(value):
    high = value.astype(jnp.bfloat16).astype(jnp.float32)
    rest = value - high
    middle = rest.astype(jnp.bfloat16).astype(jnp.float32)
    return high, middle, rest - middle


def outer_product(up, inv):
    h, m, l = three_parts(up)
    a, b, c = three_parts(inv)
    tall = jnp.concatenate([h, h, m, h, l, m], axis=0).astype(jnp.bfloat16)
    wide = jnp.concatenate([jnp.concatenate([h, m, h, l, h, m], axis=0),
                            jnp.concatenate([a, b, a, c, a, b], axis=0)], axis=1).astype(jnp.bfloat16)
    return lax.dot_general(tall, wide, (((0,), (0,)), ((), ())), preferred_element_type=jnp.float32)


NEAR = 2
FEW = 3


def factor_diagonal(block_ref, upper_ref, inverse_ref, aside):
    sub = lax.broadcasted_iota(jnp.int32, (8, 128), 0)
    lane = lax.broadcasted_iota(jnp.int32, (8, 128), 1)
    left = [block_ref[8 * i:8 * i + 8, :] for i in range(16)]
    right = [jnp.where(lane == sub + 8 * i, 1.0, 0.0).astype(jnp.float32) for i in range(16)]
    for k in range(16):
        base = 8 * k
        columns = [lanes(left[k], base + r) for r in range(8)]
        entry = {(q, r): rows(columns[r], q) for r in range(8) for q in range(r, 8)}
        u = [rows(left[k], r) for r in range(8)]
        v = [rows(right[k], r) for r in range(8)]
        scale = []
        lower = {}
        for r in range(8):
            s = lax.rsqrt(entry[r, r])
            scale.append(s)
            for q in range(r + 1, 8):
                lower[q, r] = entry[q, r] * s
            for q in range(r + 1, 8):
                for t in range(r + 1, q + 1):
                    entry[q, t] = entry[q, t] - lower[q, r] * lower[t, r]
            u[r] = u[r] * s
            v[r] = v[r] * s
            for q in range(r + 1, 8):
                u[q] = u[q] - lower[q, r] * u[r]
                v[q] = v[q] - lower[q, r] * v[r]
        up = u[0]
        inv = v[0]
        for r in range(1, 8):
            up = jnp.where(sub == r, u[r], up)
            inv = jnp.where(sub == r, v[r], inv)
        up = jnp.where(lane >= sub + base, up, 0.0)
        upper_ref[base:base + 8, :] = up
        inverse_ref[base:base + 8, :] = inv
        near = min(16, k + 1 + NEAR)
        if 16 - near < FEW:
            near = 16
        for i in range(k + 1, near):
            col = [lanes(left[i], base + r) for r in range(8)]
            for r in range(8):
                col[r] = col[r] * scale[r]
                for q in range(r + 1, 8):
                    col[q] = col[q] - lower[q, r] * col[r]
            for r in range(8):
                left[i] = left[i] - col[r] * u[r]
                right[i] = right[i] - col[r] * v[r]
        if near < 16:
            delta = outer_product(up, inv)
            for i in range(near, 16):
                left[i] = left[i] - delta[8 * i:8 * i + 8, :128]
                right[i] = right[i] - delta[8 * i:8 * i + 8, 128:]
        for work in aside[len(aside) * k // 16:len(aside) * (k + 1) // 16]:
            work()


def orthonormalize_kernel(cells, packed_ref, fields_ref, wide_ref, out_hbm, factor_hbm,
                          gram, work, out_ref, factor_ref, upper, inverse, sems):
    nb = 4
    squared = packed_ref[0, 80, 1:2, :]
    aligned = [packed_ref[j // 2, 80 + j % 2, 0:1, :] for j in range(nb)]
    weight = [a / (squared + EPSILON) for a in aligned]
    ratio = jnp.sqrt(squared + 2 * EPSILON) / (squared + EPSILON)
    removed = [a * ratio for a in aligned]

    def span(j):
        return slice(128 * j, 128 * j + 128)

    def prepare(i, j):
        b = i * (i + 1) // 2 + j
        tall = jnp.broadcast_to(removed[i], (128, 128)).T
        raw = packed_ref[:, 8 * b:8 * b + 8].reshape(128, 128)
        gram[span(i), span(j)] = (raw - tall * removed[j]) * (1.0 / cells)
        if i != j:
            factor_ref[span(j), span(i)] = jnp.zeros((128, 128), jnp.float32)

    def project(i, j):
        work[span(i), span(j)] = fields_ref[span(i), span(j)] - wide_ref[span(i)] * weight[j]

    def panel(i, j):
        factor_ref[span(i), span(j)] = dot_nt(gram[span(i), span(j)], inverse[j])

    def update(i, k, j):
        gram[span(i), span(k)] = gram[span(i), span(k)] - dot_nt(factor_ref[span(i), span(j)],
                                                                factor_ref[span(k), span(j)])

    def result(c, j):
        out_ref[span(c), span(j)] = dot_nt(work[span(c), span(j)], inverse[j])

    def remove(c, k, j):
        work[span(c), span(k)] = work[span(c), span(k)] - dot_nt(out_ref[span(c), span(j)],
                                                                factor_ref[span(k), span(j)])

    def sent(j):
        here = pl.ds(128 * j, 128)
        return pltpu.make_async_copy(out_ref.at[:, here], out_hbm.at[:, here], sems.at[j])

    factor_copy = pltpu.make_async_copy(factor_ref, factor_hbm, sems.at[nb])
    prepare(0, 0)
    aside = [functools.partial(prepare, i, j) for i in range(1, nb) for j in range(i + 1)]
    aside += [functools.partial(project, i, j) for j in range(nb) for i in range(nb)]
    for j in range(nb):
        factor_diagonal(gram.at[span(j), span(j)], upper, inverse.at[j], aside)
        factor_ref[span(j), span(j)] = upper[...].T
        aside = []
        if j + 1 < nb:
            panel(j + 1, j)
            update(j + 1, j + 1, j)
            aside += [functools.partial(panel, i, j) for i in range(j + 2, nb)]
            aside += [functools.partial(update, i, k, j) for i in range(j + 2, nb) for k in range(j + 1, i + 1)]
            aside += [functools.partial(result, c, j) for c in range(nb)]
            aside += [sent(j).start]
            aside += [functools.partial(remove, c, k, j) for k in range(j + 1, nb) for c in range(nb)]
    factor_copy.start()
    for c in range(nb):
        result(c, nb - 1)
    sent(nb - 1).start()
    for j in range(nb):
        sent(j).wait()
    factor_copy.wait()


def orthonormalize(packed, fields, wide, cells):
    n = fields.shape[0]
    vm = pl.BlockSpec(memory_space=pltpu.VMEM)
    hbm = pl.BlockSpec(memory_space=pltpu.HBM)
    return pl.pallas_call(
        functools.partial(orthonormalize_kernel, cells),
        out_shape=(jax.ShapeDtypeStruct((n, 512), jnp.float32), jax.ShapeDtypeStruct((512, 512), jnp.float32)),
        in_specs=[vm] * 3, out_specs=(hbm, hbm),
        scratch_shapes=[pltpu.VMEM((512, 512), jnp.float32), pltpu.VMEM((n, 512), jnp.float32),
                        pltpu.VMEM((n, 512), jnp.float32), pltpu.VMEM((512, 512), jnp.float32),
                        pltpu.VMEM((128, 128), jnp.float32), pltpu.VMEM((4, 128, 128), jnp.float32),
                        pltpu.SemaphoreType.DMA((5,))],
        compiler_params=pltpu.CompilerParams(vmem_limit_bytes=40 * 1024 * 1024),
    )(packed, fields, wide)


MESH = pl.DeviceIdType.MESH
TILES = 96
HALF = 48
PIECE = 6
LEVEL_OF_ROUND = (2, 1, 1, 0)


def evolve_kernel(fields_hbm, center_hbm, neighbor_hbm, neutral_hbm, evolved_ref, out_ref, wide_ref,
                  fields_ref, center_ref, neighbor_ref, neutral_ref,
                  coef, trial, late, slope, x_send, y_send, x_recv, y_recv,
                  pack, from_core, mid, from_plane, tail, from_ring,
                  in_sems, x_sems, y_sems, core_sems, plane_sems, ring_sems, back_sems):
    gx, gy = lax.axis_index("gx"), lax.axis_index("gy")
    core, y = lax.rem(gx, 2), lax.div(gx, 2)
    z, x = lax.rem(gy, 8), lax.div(gy, 8)
    other = 1 - core
    partner = (gx + 1 - 2 * core, gy)
    x_sides = ((lax.rem(gx + 1, 8), gy), (lax.rem(gx + 7, 8), gy))
    y_sides = ((gx, lax.rem(gy + 1, 32)), (gx, lax.rem(gy + 31, 32)))

    def on_plane(offset):
        peer_y, peer_x = lax.rem(y + offset[0], 4), lax.rem(x + offset[1], 4)
        return place_of(peer_y, peer_x), (2 * peer_y + core, 8 * peer_x + z)

    def place_of(at_y, at_x):
        return 8 * lax.rem(at_y + at_x, 2) + 2 * at_y + lax.div(at_x, 2)

    offsets = sorted(((a, b) for a in range(4) for b in range(4) if a or b),
                     key=lambda o: -(min(o[0], 4 - o[0]) + min(o[1], 4 - o[1])))
    place = place_of(y, x)

    def along_z(step):
        peer = lax.rem(z + step, 8)
        return peer, (gx, 8 * x + peer)

    barrier = pltpu.get_barrier_semaphore()
    greeted = [*x_sides, *y_sides, partner]
    greeted += [on_plane(offset)[1] for offset in offsets]
    greeted += [along_z(step)[1] for step in range(1, 8)]
    for device in greeted:
        pl.semaphore_signal(barrier, inc=1, device_id=device, device_id_type=MESH)
    loads = [pltpu.make_async_copy(neighbor_hbm, neighbor_ref, in_sems.at[0]),
             pltpu.make_async_copy(center_hbm, center_ref, in_sems.at[1])]
    for g in range(4):
        lanes = pl.ds(128 * g, 128)
        loads.append(pltpu.make_async_copy(fields_hbm.at[:, :, :, lanes], fields_ref.at[:, :, :, lanes],
                                           in_sems.at[2 + g]))
    loads.append(pltpu.make_async_copy(neutral_hbm, neutral_ref, in_sems.at[6]))
    for load in loads:
        load.start()

    def spread(level):
        depth = lax.broadcasted_iota(jnp.int32, (16, 128), 0)
        for component in range(7):
            if component == 0:
                table = center_ref[32 * level:32 * level + 32, :].T
            else:
                start = 192 * level + 32 * (component - 1)
                table = neighbor_ref[start:start + 32, :].T
            for cell in range(32):
                value = jnp.broadcast_to(table[:, cell:cell + 1], (16, 128))
                if component == 5:
                    value = jnp.where(depth == 15, 0.0, value)
                if component == 6:
                    value = jnp.where(depth == 0, 0.0, value)
                coef[level, component, cell // 8, cell % 8] = value

    def lanes_of(g):
        return slice(128 * g, 128 * g + 128)

    def held(r, g, i):
        if r == 0:
            return fields_ref[i, :, :, lanes_of(g)]
        if r == 2:
            return evolved_ref[128 * i:128 * i + 128, lanes_of(g)].reshape(8, 16, 128)
        return trial[g, i]

    def face_copies(r, g):
        copies = []
        for side in range(2):
            copies.append(pltpu.make_async_remote_copy(
                src_ref=x_send.at[r, g, side], dst_ref=x_recv.at[r, g, side],
                send_sem=x_sems.at[0, r, g, side], recv_sem=x_sems.at[1, r, g, side],
                device_id=x_sides[side], device_id_type=MESH))
            copies.append(pltpu.make_async_remote_copy(
                src_ref=y_send.at[r, g, side], dst_ref=y_recv.at[r, g, side],
                send_sem=y_sems.at[0, r, g, side], recv_sem=y_sems.at[1, r, g, side],
                device_id=y_sides[side], device_id_type=MESH))
        return copies

    def send_faces(r, g):
        level = LEVEL_OF_ROUND[r]
        copies = face_copies(r, g)
        x_edge = (gx < 7, gx > 0)
        y_edge = (gy < 31, gy > 0)
        for side in range(2):
            i = (3, 0)[side]
            x_send[r, g, side] = jnp.where(x_edge[side], coef[level, 1 + side, i] * held(r, g, i), 0.0)
            copies[2 * side].start()
        for side in range(2):
            j = (7, 0)[side]
            for i in range(4):
                value = held(r, g, i)[j]
                y_send[r, g, side, i] = jnp.where(y_edge[side], coef[level, 3 + side, i, j] * value, 0.0)
            copies[2 * side + 1].start()

    def local_terms(r, g):
        level = LEVEL_OF_ROUND[r]
        for i in range(4):
            v = held(r, g, i)
            total = coef[level, 0, i] * v
            up = (coef[level, 5, i] * v).reshape(128, 128)
            down = (coef[level, 6, i] * v).reshape(128, 128)
            total = total + pltpu.roll(up, 1, 0).reshape(8, 16, 128)
            total = total + pltpu.roll(down, 127, 0).reshape(8, 16, 128)
            if i > 0:
                total = total + coef[level, 1, i - 1] * held(r, g, i - 1)
            if i < 3:
                total = total + coef[level, 2, i + 1] * held(r, g, i + 1)
            zero = jnp.zeros((1, 16, 128), jnp.float32)
            total = total + jnp.concatenate([zero, (coef[level, 3, i] * v)[:7]], axis=0)
            total = total + jnp.concatenate([(coef[level, 4, i] * v)[1:], zero], axis=0)
            slope[g, i] = total

    def finish(r, g):
        parts = []
        for c in face_copies(r, g):
            c.wait()
        for i in range(4):
            total = slope[g, i]
            if i == 0:
                total = total + x_recv[r, g, 0]
            if i == 3:
                total = total + x_recv[r, g, 1]
            total = jnp.concatenate([(total[0] + y_recv[r, g, 0, i])[None], total[1:7],
                                     (total[7] + y_recv[r, g, 1, i])[None]], axis=0)
            start = held(0 if r < 2 else 2, g, i)
            if r % 2 == 0:
                late[g, i] = total
                trial[g, i] = start + STEP_SIZE * total
            else:
                done = start + 0.5 * STEP_SIZE * (late[g, i] + total)
                evolved_ref[128 * i:128 * i + 128, lanes_of(g)] = done.reshape(128, 128)
                if r == 3:
                    parts.append(jnp.sum(done.reshape(16, 8, 128) * wide_ref[128 * i:128 * i + 128].reshape(16, 8, 128),
                                         axis=0))
        return parts

    def copy(src, dst, sems, mine, theirs, device):
        return pltpu.make_async_remote_copy(src_ref=src, dst_ref=dst, send_sem=sems.at[0, theirs],
                                            recv_sem=sems.at[1, mine], device_id=device, device_id_type=MESH)

    def core_copy(b):
        span = pl.ds(8 * b, 8) if b < 10 else pl.ds(80, 2)
        return copy(pack.at[other, span], from_core.at[span], core_sems, b, b, partner)

    def plane_start(wave):
        for offset in offsets:
            peer, device = on_plane(offset)

            @pl.when(lax.div(peer, 8) == wave)
            def _():
                copy(mid.at[pl.ds(peer * PIECE, PIECE)], from_plane.at[place], plane_sems, place, peer,
                     device).start()

    loads[0].wait()
    loads[1].wait()
    spread(2)
    pl.semaphore_wait(barrier, len(greeted))
    for r in range(4):
        for g in range(4):
            if r > 0:
                finish(r - 1, g)
            else:
                loads[2 + g].wait()
            send_faces(r, g)
            local_terms(r, g)
        if r < 2:
            spread(1 - r)
        if r == 2:
            loads[6].wait()
            table = neutral_ref[...].T
            for cell in range(32):
                wide_ref[16 * cell:16 * cell + 16] = jnp.broadcast_to(table[:, cell:cell + 1], (16, 128))

    sub = lax.broadcasted_iota(jnp.int32, (8, 128), 0)
    squared = jnp.sum(neutral_ref[...] * neutral_ref[...])
    for g in range(4):
        parts = finish(3, g)
        product = lax.dot_general(evolved_ref[:, lanes_of(g)], evolved_ref[:, :128 * g + 128],
                                  (((0,), (0,)), ((), ())), precision=HIGHEST,
                                  preferred_element_type=jnp.float32)
        for j in range(g + 1):
            b = g * (g + 1) // 2 + j
            pack[:, 8 * b:8 * b + 8] = product[:, 128 * j:128 * j + 128].reshape(2, 8, 8, 128)
            core_copy(b).start()
        aligned = jnp.sum(parts[0] + parts[1] + (parts[2] + parts[3]), axis=0, keepdims=True)
        pack[g // 2, 80 + g % 2] = jnp.where(sub == 1, squared, aligned)
        if g == 2:
            for b in range(6):
                core_copy(b).wait()
            mid[0:HALF] = pack[core, 0:HALF] + from_core[0:HALF]
            plane_start(0)
    core_copy(10).start()
    for b in range(6, 11):
        core_copy(b).wait()
    mid[HALF:82] = pack[core, HALF:82] + from_core[HALF:82]
    mid[82:TILES] = jnp.zeros((TILES - 82, 8, 128), jnp.float32)
    plane_start(1)

    total = mid[pl.ds(place * PIECE, PIECE)]
    for offset in reversed(offsets):
        peer, device = on_plane(offset)
        copy(mid.at[pl.ds(peer * PIECE, PIECE)], from_plane.at[peer], plane_sems, peer, peer, device).wait()
        total = total + from_plane[peer]
    tail[...] = total
    for step in (4, 3, 5, 2, 6, 1, 7):
        peer, device = along_z(step)
        copy(tail, from_ring.at[z], ring_sems, z, peer, device).start()
    from_ring[z] = total
    for step in (1, 7, 2, 6, 3, 5, 4):
        peer, device = along_z(step)
        copy(tail, from_ring.at[peer], ring_sems, peer, peer, device).wait()
    final = from_ring[0]
    for p in range(1, 8):
        final = final + from_ring[p]

    def back(side, owner, device):
        spot = out_ref.at[side, pl.ds(owner * PIECE, PIECE)]
        return copy(spot, spot, back_sems, owner, owner, device)

    def forward(side, owner):
        spot = out_ref.at[side, pl.ds(owner * PIECE, PIECE)]
        return copy(spot, spot, back_sems, 16 + owner, 16 + owner, partner)

    out_ref[core, pl.ds(place * PIECE, PIECE)] = final
    for offset in offsets:
        peer, device = on_plane(offset)
        spot = out_ref.at[core, pl.ds(place * PIECE, PIECE)]
        copy(spot, spot, back_sems, place, peer, device).start()
    forward(core, place).start()
    for offset in reversed(offsets):
        peer, device = on_plane(offset)
        back(core, peer, device).wait()
        forward(core, peer).start()
    for owner in range(16):
        forward(other, owner).wait()


def evolve_and_reduce(fields, center, neighbor, neutral):
    vm = pl.BlockSpec(memory_space=pltpu.VMEM)
    hbm = pl.BlockSpec(memory_space=pltpu.HBM)

    def tiles(*lead):
        return pltpu.VMEM((*lead, 8, 128), jnp.float32)

    def columns(*lead):
        return pltpu.VMEM((*lead, 16, 128), jnp.float32)

    arguments = (fields, center, neighbor, neutral)
    return pl.pallas_call(
        evolve_kernel,
        out_shape=(jax.ShapeDtypeStruct((512, 512), jnp.float32),
                   jax.ShapeDtypeStruct((2, TILES, 8, 128), jnp.float32),
                   jax.ShapeDtypeStruct((512, 128), jnp.float32)),
        in_specs=[hbm] * 4, out_specs=(vm, vm, vm),
        scratch_shapes=[
            *[pltpu.VMEM(a.shape, jnp.float32) for a in arguments],
            columns(3, 7, 4, 8), columns(4, 4, 8), columns(4, 4, 8), columns(4, 4, 8),
            columns(4, 4, 2, 8), columns(4, 4, 2, 4), columns(4, 4, 2, 8), columns(4, 4, 2, 4),
            tiles(2, TILES), tiles(TILES), tiles(TILES), tiles(16, PIECE), tiles(PIECE), tiles(8, PIECE),
            pltpu.SemaphoreType.DMA((7,)),
            pltpu.SemaphoreType.DMA((2, 4, 4, 2)), pltpu.SemaphoreType.DMA((2, 4, 4, 2)),
            pltpu.SemaphoreType.DMA((2, 11)), pltpu.SemaphoreType.DMA((2, 16)),
            pltpu.SemaphoreType.DMA((2, 8)), pltpu.SemaphoreType.DMA((2, 32)),
        ],
        compiler_params=pltpu.CompilerParams(collective_id=1, has_side_effects=True,
                                             vmem_limit_bytes=103 * 512 * 1024),
    )(*arguments)


def shards(adjoint_fields, center_coef, neighbor_coef, neutral):
    cells_x, cells_y, depth_cells, columns = adjoint_fields.shape
    cell_count = cells_x * lax.axis_size("gx") * cells_y * lax.axis_size("gy") * depth_cells
    evolved, packed, wide = evolve_and_reduce(
        adjoint_fields, center_coef.reshape(-1, depth_cells), neighbor_coef.reshape(-1, depth_cells),
        neutral.reshape(-1, depth_cells))
    orthonormal, factor = orthonormalize(packed, evolved, wide, cell_count)
    return (orthonormal.reshape(adjoint_fields.shape), factor)


def solution(mesh):
    in_specs = (
        P("gx", "gy", None, None),
        P(None, "gx", "gy", None),
        P(None, None, "gx", "gy", None),
        P("gx", "gy", None),
    )
    out_specs = (P("gx", "gy", None, None), P())
    return jax.shard_map(shards, mesh=mesh, in_specs=in_specs, out_specs=out_specs, check_vma=False)
```

```python
import functools

import jax
import jax.numpy as jnp
from jax import lax
from jax.experimental import pallas as pl
from jax.experimental.pallas import tpu as pltpu
from jax.sharding import PartitionSpec as P

STEP_SIZE = 0.15
EPSILON = 1e-06
HIGHEST = lax.Precision.HIGHEST


def dot_nt(a, b):
    return lax.dot_general(a, b, (((1,), (1,)), ((), ())), precision=HIGHEST,
                           preferred_element_type=jnp.float32)


def lanes(value, column):
    return jnp.broadcast_to(value[:, column:column + 1], (8, 128))


def rows(value, row):
    return jnp.broadcast_to(value[row:row + 1, :], (8, 128))


def three_parts(value):
    high = value.astype(jnp.bfloat16).astype(jnp.float32)
    rest = value - high
    middle = rest.astype(jnp.bfloat16).astype(jnp.float32)
    return high, middle, rest - middle


def outer_product(up, inv):
    h, m, l = three_parts(up)
    a, b, c = three_parts(inv)
    tall = jnp.concatenate([h, h, m, h, l, m], axis=0).astype(jnp.bfloat16)
    wide = jnp.concatenate([jnp.concatenate([h, m, h, l, h, m], axis=0),
                            jnp.concatenate([a, b, a, c, a, b], axis=0)], axis=1).astype(jnp.bfloat16)
    return lax.dot_general(tall, wide, (((0,), (0,)), ((), ())), preferred_element_type=jnp.float32)


NEAR = 2
FEW = 3


def factor_diagonal(block_ref, upper_ref, inverse_ref, aside):
    sub = lax.broadcasted_iota(jnp.int32, (8, 128), 0)
    lane = lax.broadcasted_iota(jnp.int32, (8, 128), 1)
    left = [block_ref[8 * i:8 * i + 8, :] for i in range(16)]
    right = [jnp.where(lane == sub + 8 * i, 1.0, 0.0).astype(jnp.float32) for i in range(16)]
    for k in range(16):
        base = 8 * k
        columns = [lanes(left[k], base + r) for r in range(8)]
        entry = {(q, r): rows(columns[r], q) for r in range(8) for q in range(r, 8)}
        u = [rows(left[k], r) for r in range(8)]
        v = [rows(right[k], r) for r in range(8)]
        scale = []
        lower = {}
        for r in range(8):
            s = lax.rsqrt(entry[r, r])
            scale.append(s)
            for q in range(r + 1, 8):
                lower[q, r] = entry[q, r] * s
            for q in range(r + 1, 8):
                for t in range(r + 1, q + 1):
                    entry[q, t] = entry[q, t] - lower[q, r] * lower[t, r]
            u[r] = u[r] * s
            v[r] = v[r] * s
            for q in range(r + 1, 8):
                u[q] = u[q] - lower[q, r] * u[r]
                v[q] = v[q] - lower[q, r] * v[r]
        up = u[0]
        inv = v[0]
        for r in range(1, 8):
            up = jnp.where(sub == r, u[r], up)
            inv = jnp.where(sub == r, v[r], inv)
        up = jnp.where(lane >= sub + base, up, 0.0)
        upper_ref[base:base + 8, :] = up
        inverse_ref[base:base + 8, :] = inv
        near = min(16, k + 1 + NEAR)
        if 16 - near < FEW:
            near = 16
        for i in range(k + 1, near):
            col = [lanes(left[i], base + r) for r in range(8)]
            for r in range(8):
                col[r] = col[r] * scale[r]
                for q in range(r + 1, 8):
                    col[q] = col[q] - lower[q, r] * col[r]
            for r in range(8):
                left[i] = left[i] - col[r] * u[r]
                right[i] = right[i] - col[r] * v[r]
        if near < 16:
            delta = outer_product(up, inv)
            for i in range(near, 16):
                left[i] = left[i] - delta[8 * i:8 * i + 8, :128]
                right[i] = right[i] - delta[8 * i:8 * i + 8, 128:]
        for work in aside[len(aside) * k // 16:len(aside) * (k + 1) // 16]:
            work()


def orthonormalize_kernel(cells, packed_ref, fields_ref, wide_ref, out_hbm, factor_hbm,
                          gram, work, out_ref, factor_ref, upper, inverse, sems):
    nb = 4
    lane = lax.broadcasted_iota(jnp.int32, (8, 128), 1)

    def carried(j, row):
        tile = packed_ref[0, 4 * j * (j + 3), row:row + 1, :]
        return jnp.broadcast_to(tile, (8, 128))

    turned = pltpu.roll(carried(0, 2), 64, 1)
    squared = jnp.where(lane < 64, turned, carried(0, 2))[0:1]
    aligned = [jnp.where(lane < 64, pltpu.roll(carried(j, 1), 64, 1), carried(j, 0))[0:1] for j in range(nb)]
    weight = [a / (squared + EPSILON) for a in aligned]
    ratio = jnp.sqrt(squared + 2 * EPSILON) / (squared + EPSILON)
    removed = [a * ratio for a in aligned]

    def span(j):
        return slice(128 * j, 128 * j + 128)

    def prepare(i, j):
        b = i * (i + 1) // 2 + j
        tall = jnp.broadcast_to(removed[i], (128, 128)).T
        raw = packed_ref[:, 8 * b:8 * b + 8].reshape(128, 128)
        if i == j:
            top = jnp.where(lane < 64, raw[:8], raw.T[:8])
            raw = jnp.concatenate([top, raw[8:]], axis=0)
        gram[span(i), span(j)] = (raw - tall * removed[j]) * (1.0 / cells)
        if i != j:
            factor_ref[span(j), span(i)] = jnp.zeros((128, 128), jnp.float32)

    def project(i, j):
        work[span(i), span(j)] = fields_ref[span(i), span(j)] - wide_ref[span(i)] * weight[j]

    def panel(i, j):
        factor_ref[span(i), span(j)] = dot_nt(gram[span(i), span(j)], inverse[j])

    def update(i, k, j):
        gram[span(i), span(k)] = gram[span(i), span(k)] - dot_nt(factor_ref[span(i), span(j)],
                                                                factor_ref[span(k), span(j)])

    def result(c, j):
        out_ref[span(c), span(j)] = dot_nt(work[span(c), span(j)], inverse[j])

    def remove(c, k, j):
        work[span(c), span(k)] = work[span(c), span(k)] - dot_nt(out_ref[span(c), span(j)],
                                                                factor_ref[span(k), span(j)])

    def sent(j):
        here = pl.ds(128 * j, 128)
        return pltpu.make_async_copy(out_ref.at[:, here], out_hbm.at[:, here], sems.at[j])

    factor_copy = pltpu.make_async_copy(factor_ref, factor_hbm, sems.at[nb])
    prepare(0, 0)
    aside = [functools.partial(prepare, i, j) for i in range(1, nb) for j in range(i + 1)]
    aside += [functools.partial(project, i, j) for j in range(nb) for i in range(nb)]
    for j in range(nb):
        factor_diagonal(gram.at[span(j), span(j)], upper, inverse.at[j], aside)
        factor_ref[span(j), span(j)] = upper[...].T
        aside = []
        if j + 1 < nb:
            panel(j + 1, j)
            update(j + 1, j + 1, j)
            aside += [functools.partial(panel, i, j) for i in range(j + 2, nb)]
            aside += [functools.partial(update, i, k, j) for i in range(j + 2, nb) for k in range(j + 1, i + 1)]
            aside += [functools.partial(result, c, j) for c in range(nb)]
            aside += [sent(j).start]
            aside += [functools.partial(remove, c, k, j) for k in range(j + 1, nb) for c in range(nb)]
    factor_copy.start()
    for c in range(nb):
        result(c, nb - 1)
    sent(nb - 1).start()
    for j in range(nb):
        sent(j).wait()
    factor_copy.wait()


def orthonormalize(packed, fields, wide, cells):
    n = fields.shape[0]
    vm = pl.BlockSpec(memory_space=pltpu.VMEM)
    hbm = pl.BlockSpec(memory_space=pltpu.HBM)
    return pl.pallas_call(
        functools.partial(orthonormalize_kernel, cells),
        out_shape=(jax.ShapeDtypeStruct((n, 512), jnp.float32), jax.ShapeDtypeStruct((512, 512), jnp.float32)),
        in_specs=[vm] * 3, out_specs=(hbm, hbm),
        scratch_shapes=[pltpu.VMEM((512, 512), jnp.float32), pltpu.VMEM((n, 512), jnp.float32),
                        pltpu.VMEM((n, 512), jnp.float32), pltpu.VMEM((512, 512), jnp.float32),
                        pltpu.VMEM((128, 128), jnp.float32), pltpu.VMEM((4, 128, 128), jnp.float32),
                        pltpu.SemaphoreType.DMA((5,))],
        compiler_params=pltpu.CompilerParams(vmem_limit_bytes=40 * 1024 * 1024),
    )(packed, fields, wide)


MESH = pl.DeviceIdType.MESH
TILES = 80
HALF = 40
PIECE = 5
LEVEL_OF_ROUND = (2, 1, 1, 0)


def evolve_kernel(fields_hbm, center_hbm, neighbor_hbm, neutral_hbm, evolved_ref, out_ref, wide_ref,
                  fields_ref, center_ref, neighbor_ref, neutral_ref,
                  coef, trial, late, slope, x_send, y_send, x_recv, y_recv,
                  pack, from_core, mid, from_plane, tail, from_ring,
                  in_sems, x_sems, y_sems, core_sems, plane_sems, ring_sems, back_sems):
    gx, gy = lax.axis_index("gx"), lax.axis_index("gy")
    core, y = lax.rem(gx, 2), lax.div(gx, 2)
    z, x = lax.rem(gy, 8), lax.div(gy, 8)
    other = 1 - core
    partner = (gx + 1 - 2 * core, gy)
    x_sides = ((lax.rem(gx + 1, 8), gy), (lax.rem(gx + 7, 8), gy))
    y_sides = ((gx, lax.rem(gy + 1, 32)), (gx, lax.rem(gy + 31, 32)))

    def on_plane(offset):
        peer_y, peer_x = lax.rem(y + offset[0], 4), lax.rem(x + offset[1], 4)
        return place_of(peer_y, peer_x), (2 * peer_y + core, 8 * peer_x + z)

    def place_of(at_y, at_x):
        return 8 * lax.rem(at_y + at_x, 2) + 2 * at_y + lax.div(at_x, 2)

    offsets = sorted(((a, b) for a in range(4) for b in range(4) if a or b),
                     key=lambda o: -(min(o[0], 4 - o[0]) + min(o[1], 4 - o[1])))
    place = place_of(y, x)

    def along_z(step):
        peer = lax.rem(z + step, 8)
        return peer, (gx, 8 * x + peer)

    barrier = pltpu.get_barrier_semaphore()
    greeted = [*x_sides, *y_sides, partner]
    greeted += [on_plane(offset)[1] for offset in offsets]
    greeted += [along_z(step)[1] for step in range(1, 8)]
    for device in greeted:
        pl.semaphore_signal(barrier, inc=1, device_id=device, device_id_type=MESH)
    loads = [pltpu.make_async_copy(neighbor_hbm, neighbor_ref, in_sems.at[0]),
             pltpu.make_async_copy(center_hbm, center_ref, in_sems.at[1])]
    for g in range(4):
        lanes = pl.ds(128 * g, 128)
        loads.append(pltpu.make_async_copy(fields_hbm.at[:, :, :, lanes], fields_ref.at[:, :, :, lanes],
                                           in_sems.at[2 + g]))
    loads.append(pltpu.make_async_copy(neutral_hbm, neutral_ref, in_sems.at[6]))
    for load in loads:
        load.start()

    def spread(level):
        depth = lax.broadcasted_iota(jnp.int32, (16, 128), 0)
        for component in range(7):
            if component == 0:
                table = center_ref[32 * level:32 * level + 32, :].T
            else:
                start = 192 * level + 32 * (component - 1)
                table = neighbor_ref[start:start + 32, :].T
            for cell in range(32):
                value = jnp.broadcast_to(table[:, cell:cell + 1], (16, 128))
                if component == 5:
                    value = jnp.where(depth == 15, 0.0, value)
                if component == 6:
                    value = jnp.where(depth == 0, 0.0, value)
                coef[level, component, cell // 8, cell % 8] = value

    def lanes_of(g):
        return slice(128 * g, 128 * g + 128)

    def held(r, g, i):
        if r == 0:
            return fields_ref[i, :, :, lanes_of(g)]
        if r == 2:
            return evolved_ref[128 * i:128 * i + 128, lanes_of(g)].reshape(8, 16, 128)
        return trial[g, i]

    def face_copies(r, g):
        copies = []
        for side in range(2):
            copies.append(pltpu.make_async_remote_copy(
                src_ref=x_send.at[r, g, side], dst_ref=x_recv.at[r, g, side],
                send_sem=x_sems.at[0, r, g, side], recv_sem=x_sems.at[1, r, g, side],
                device_id=x_sides[side], device_id_type=MESH))
            copies.append(pltpu.make_async_remote_copy(
                src_ref=y_send.at[r, g, side], dst_ref=y_recv.at[r, g, side],
                send_sem=y_sems.at[0, r, g, side], recv_sem=y_sems.at[1, r, g, side],
                device_id=y_sides[side], device_id_type=MESH))
        return copies

    def send_faces(r, g):
        level = LEVEL_OF_ROUND[r]
        copies = face_copies(r, g)
        x_edge = (gx < 7, gx > 0)
        y_edge = (gy < 31, gy > 0)
        for side in range(2):
            i = (3, 0)[side]
            x_send[r, g, side] = jnp.where(x_edge[side], coef[level, 1 + side, i] * held(r, g, i), 0.0)
            copies[2 * side].start()
        for side in range(2):
            j = (7, 0)[side]
            for i in range(4):
                value = held(r, g, i)[j]
                y_send[r, g, side, i] = jnp.where(y_edge[side], coef[level, 3 + side, i, j] * value, 0.0)
            copies[2 * side + 1].start()

    def local_terms(r, g):
        level = LEVEL_OF_ROUND[r]
        for i in range(4):
            v = held(r, g, i)
            total = coef[level, 0, i] * v
            up = (coef[level, 5, i] * v).reshape(128, 128)
            down = (coef[level, 6, i] * v).reshape(128, 128)
            total = total + pltpu.roll(up, 1, 0).reshape(8, 16, 128)
            total = total + pltpu.roll(down, 127, 0).reshape(8, 16, 128)
            if i > 0:
                total = total + coef[level, 1, i - 1] * held(r, g, i - 1)
            if i < 3:
                total = total + coef[level, 2, i + 1] * held(r, g, i + 1)
            zero = jnp.zeros((1, 16, 128), jnp.float32)
            total = total + jnp.concatenate([zero, (coef[level, 3, i] * v)[:7]], axis=0)
            total = total + jnp.concatenate([(coef[level, 4, i] * v)[1:], zero], axis=0)
            slope[g, i] = total

    def finish(r, g):
        parts = []
        for c in face_copies(r, g):
            c.wait()
        for i in range(4):
            total = slope[g, i]
            if i == 0:
                total = total + x_recv[r, g, 0]
            if i == 3:
                total = total + x_recv[r, g, 1]
            total = jnp.concatenate([(total[0] + y_recv[r, g, 0, i])[None], total[1:7],
                                     (total[7] + y_recv[r, g, 1, i])[None]], axis=0)
            start = held(0 if r < 2 else 2, g, i)
            if r % 2 == 0:
                late[g, i] = total
                trial[g, i] = start + STEP_SIZE * total
            else:
                done = start + 0.5 * STEP_SIZE * (late[g, i] + total)
                evolved_ref[128 * i:128 * i + 128, lanes_of(g)] = done.reshape(128, 128)
                if r == 3:
                    parts.append(jnp.sum(done.reshape(16, 8, 128) * wide_ref[128 * i:128 * i + 128].reshape(16, 8, 128),
                                         axis=0))
        return parts

    def copy(src, dst, sems, mine, theirs, device):
        return pltpu.make_async_remote_copy(src_ref=src, dst_ref=dst, send_sem=sems.at[0, theirs],
                                            recv_sem=sems.at[1, mine], device_id=device, device_id_type=MESH)

    def core_copy(b):
        span = pl.ds(8 * b, 8)
        return copy(pack.at[other, span], from_core.at[span], core_sems, b, b, partner)

    def plane_start(wave):
        for offset in offsets:
            peer, device = on_plane(offset)

            @pl.when(lax.div(peer, 8) == wave)
            def _():
                copy(mid.at[pl.ds(peer * PIECE, PIECE)], from_plane.at[place], plane_sems, place, peer,
                     device).start()

    loads[0].wait()
    loads[1].wait()
    spread(2)
    pl.semaphore_wait(barrier, len(greeted))
    for r in range(4):
        for g in range(4):
            if r > 0:
                finish(r - 1, g)
            else:
                loads[2 + g].wait()
            send_faces(r, g)
            local_terms(r, g)
        if r < 2:
            spread(1 - r)
        if r == 2:
            loads[6].wait()
            table = neutral_ref[...].T
            for cell in range(32):
                wide_ref[16 * cell:16 * cell + 16] = jnp.broadcast_to(table[:, cell:cell + 1], (16, 128))

    sub = lax.broadcasted_iota(jnp.int32, (8, 128), 0)
    lane = lax.broadcasted_iota(jnp.int32, (8, 128), 1)
    squared = jnp.sum(neutral_ref[...] * neutral_ref[...])
    for g in range(4):
        parts = finish(3, g)
        product = lax.dot_general(evolved_ref[:, lanes_of(g)], evolved_ref[:, :128 * g + 128],
                                  (((0,), (0,)), ((), ())), precision=HIGHEST,
                                  preferred_element_type=jnp.float32)
        for j in range(g + 1):
            b = g * (g + 1) // 2 + j
            pack[:, 8 * b:8 * b + 8] = product[:, 128 * j:128 * j + 128].reshape(2, 8, 8, 128)
            if j == g:
                aligned = jnp.sum(parts[0] + parts[1] + (parts[2] + parts[3]), axis=0, keepdims=True)
                aligned = jnp.broadcast_to(aligned, (8, 128))
                carried = jnp.where(sub == 0, aligned, jnp.where(sub == 1, pltpu.roll(aligned, 64, 1), squared))
                pack[0, 8 * b] = jnp.where((lane >= 64) & (sub < 3), carried, product[:8, 128 * j:128 * j + 128])
            core_copy(b).start()
        if g == 2:
            for b in range(5):
                core_copy(b).wait()
            mid[0:HALF] = pack[core, 0:HALF] + from_core[0:HALF]
            plane_start(0)
    for b in range(5, 10):
        core_copy(b).wait()
    mid[HALF:TILES] = pack[core, HALF:TILES] + from_core[HALF:TILES]
    plane_start(1)

    total = mid[pl.ds(place * PIECE, PIECE)]
    for offset in reversed(offsets):
        peer, device = on_plane(offset)
        copy(mid.at[pl.ds(peer * PIECE, PIECE)], from_plane.at[peer], plane_sems, peer, peer, device).wait()
        total = total + from_plane[peer]
    tail[...] = total
    for step in (4, 3, 5, 2, 6, 1, 7):
        peer, device = along_z(step)
        copy(tail, from_ring.at[z], ring_sems, z, peer, device).start()
    from_ring[z] = total
    for step in (1, 7, 2, 6, 3, 5, 4):
        peer, device = along_z(step)
        copy(tail, from_ring.at[peer], ring_sems, peer, peer, device).wait()
    final = from_ring[0]
    for p in range(1, 8):
        final = final + from_ring[p]

    def back(side, owner, device):
        spot = out_ref.at[side, pl.ds(owner * PIECE, PIECE)]
        return copy(spot, spot, back_sems, owner, owner, device)

    def forward(side, owner):
        spot = out_ref.at[side, pl.ds(owner * PIECE, PIECE)]
        return copy(spot, spot, back_sems, 16 + owner, 16 + owner, partner)

    out_ref[core, pl.ds(place * PIECE, PIECE)] = final
    for offset in offsets:
        peer, device = on_plane(offset)
        spot = out_ref.at[core, pl.ds(place * PIECE, PIECE)]
        copy(spot, spot, back_sems, place, peer, device).start()
    forward(core, place).start()
    for offset in reversed(offsets):
        peer, device = on_plane(offset)
        back(core, peer, device).wait()
        forward(core, peer).start()
    for owner in range(16):
        forward(other, owner).wait()


def evolve_and_reduce(fields, center, neighbor, neutral):
    vm = pl.BlockSpec(memory_space=pltpu.VMEM)
    hbm = pl.BlockSpec(memory_space=pltpu.HBM)

    def tiles(*lead):
        return pltpu.VMEM((*lead, 8, 128), jnp.float32)

    def columns(*lead):
        return pltpu.VMEM((*lead, 16, 128), jnp.float32)

    arguments = (fields, center, neighbor, neutral)
    return pl.pallas_call(
        evolve_kernel,
        out_shape=(jax.ShapeDtypeStruct((512, 512), jnp.float32),
                   jax.ShapeDtypeStruct((2, TILES, 8, 128), jnp.float32),
                   jax.ShapeDtypeStruct((512, 128), jnp.float32)),
        in_specs=[hbm] * 4, out_specs=(vm, vm, vm),
        scratch_shapes=[
            *[pltpu.VMEM(a.shape, jnp.float32) for a in arguments],
            columns(3, 7, 4, 8), columns(4, 4, 8), columns(4, 4, 8), columns(4, 4, 8),
            columns(4, 4, 2, 8), columns(4, 4, 2, 4), columns(4, 4, 2, 8), columns(4, 4, 2, 4),
            tiles(2, TILES), tiles(TILES), tiles(TILES), tiles(16, PIECE), tiles(PIECE), tiles(8, PIECE),
            pltpu.SemaphoreType.DMA((7,)),
            pltpu.SemaphoreType.DMA((2, 4, 4, 2)), pltpu.SemaphoreType.DMA((2, 4, 4, 2)),
            pltpu.SemaphoreType.DMA((2, 10)), pltpu.SemaphoreType.DMA((2, 16)),
            pltpu.SemaphoreType.DMA((2, 8)), pltpu.SemaphoreType.DMA((2, 32)),
        ],
        compiler_params=pltpu.CompilerParams(collective_id=1, has_side_effects=True,
                                             vmem_limit_bytes=103 * 512 * 1024),
    )(*arguments)


def shards(adjoint_fields, center_coef, neighbor_coef, neutral):
    cells_x, cells_y, depth_cells, columns = adjoint_fields.shape
    cell_count = cells_x * lax.axis_size("gx") * cells_y * lax.axis_size("gy") * depth_cells
    evolved, packed, wide = evolve_and_reduce(
        adjoint_fields, center_coef.reshape(-1, depth_cells), neighbor_coef.reshape(-1, depth_cells),
        neutral.reshape(-1, depth_cells))
    orthonormal, factor = orthonormalize(packed, evolved, wide, cell_count)
    return (orthonormal.reshape(adjoint_fields.shape), factor)


def solution(mesh):
    in_specs = (
        P("gx", "gy", None, None),
        P(None, "gx", "gy", None),
        P(None, None, "gx", "gy", None),
        P("gx", "gy", None),
    )
    out_specs = (P("gx", "gy", None, None), P())
    return jax.shard_map(shards, mesh=mesh, in_specs=in_specs, out_specs=out_specs, check_vma=False)
```

```python
import functools

import jax
import jax.numpy as jnp
from jax import lax
from jax.experimental import pallas as pl
from jax.experimental.pallas import tpu as pltpu
from jax.sharding import PartitionSpec as P

STEP_SIZE = 0.15
EPSILON = 1e-06
HIGHEST = lax.Precision.HIGHEST


def dot_nt(a, b):
    return lax.dot_general(a, b, (((1,), (1,)), ((), ())), precision=HIGHEST,
                           preferred_element_type=jnp.float32)


def lanes(value, column):
    return jnp.broadcast_to(value[:, column:column + 1], (8, 128))


def rows(value, row):
    return jnp.broadcast_to(value[row:row + 1, :], (8, 128))


def three_parts(value):
    high = value.astype(jnp.bfloat16).astype(jnp.float32)
    rest = value - high
    middle = rest.astype(jnp.bfloat16).astype(jnp.float32)
    return high, middle, rest - middle


def outer_product(up, inv):
    h, m, l = three_parts(up)
    a, b, c = three_parts(inv)
    tall = jnp.concatenate([h, h, m, h, l, m], axis=0).astype(jnp.bfloat16)
    wide = jnp.concatenate([jnp.concatenate([h, m, h, l, h, m], axis=0),
                            jnp.concatenate([a, b, a, c, a, b], axis=0)], axis=1).astype(jnp.bfloat16)
    return lax.dot_general(tall, wide, (((0,), (0,)), ((), ())), preferred_element_type=jnp.float32)


NEAR = 2
FEW = 3


def factor_diagonal(block_ref, upper_ref, inverse_ref, aside):
    sub = lax.broadcasted_iota(jnp.int32, (8, 128), 0)
    lane = lax.broadcasted_iota(jnp.int32, (8, 128), 1)
    left = [block_ref[8 * i:8 * i + 8, :] for i in range(16)]
    right = [jnp.where(lane == sub + 8 * i, 1.0, 0.0).astype(jnp.float32) for i in range(16)]
    columns = [lanes(left[0], r) for r in range(8)]
    beside = None
    for k in range(16):
        base = 8 * k
        entry = {(q, r): rows(columns[r], q) for r in range(8) for q in range(r, 8)}
        u = [rows(left[k], r) for r in range(8)]
        v = [rows(right[k], r) for r in range(8)]
        scale = []
        lower = {}
        for r in range(8):
            s = lax.rsqrt(entry[r, r])
            scale.append(s)
            for q in range(r + 1, 8):
                lower[q, r] = entry[q, r] * s
            for q in range(r + 1, 8):
                for t in range(r + 1, q + 1):
                    entry[q, t] = entry[q, t] - lower[q, r] * lower[t, r]
            u[r] = u[r] * s
            v[r] = v[r] * s
            for q in range(r + 1, 8):
                u[q] = u[q] - lower[q, r] * u[r]
                v[q] = v[q] - lower[q, r] * v[r]
        up = u[0]
        inv = v[0]
        for r in range(1, 8):
            up = jnp.where(sub == r, u[r], up)
            inv = jnp.where(sub == r, v[r], inv)
        up = jnp.where(lane >= sub + base, up, 0.0)
        upper_ref[base:base + 8, :] = up
        inverse_ref[base:base + 8, :] = inv
        near = min(16, k + 1 + NEAR)
        if 16 - near < FEW:
            near = 16
        for i in range(k + 1, near):
            if beside is not None and i == k + 1:
                col = list(beside)
            else:
                col = [lanes(left[i], base + r) for r in range(8)]
            if i <= k + 1:
                after = [lanes(left[i], base + 8 + r) for r in range(8)]
            for r in range(8):
                col[r] = col[r] * scale[r]
                for q in range(r + 1, 8):
                    col[q] = col[q] - lower[q, r] * col[r]
            if i == k + 1:
                spread = [[rows(col[r], t) for t in range(8)] for r in range(8)]
                beside = None
            if i <= k + 1:
                for r in range(8):
                    for t in range(8):
                        after[t] = after[t] - col[r] * spread[r][t]
                if i == k + 1:
                    columns = after
                else:
                    beside = after
            for r in range(8):
                left[i] = left[i] - col[r] * u[r]
                right[i] = right[i] - col[r] * v[r]
        if near < 16:
            delta = outer_product(up, inv)
            for i in range(near, 16):
                left[i] = left[i] - delta[8 * i:8 * i + 8, :128]
                right[i] = right[i] - delta[8 * i:8 * i + 8, 128:]
        for work in aside[len(aside) * k // 16:len(aside) * (k + 1) // 16]:
            work()


def orthonormalize_kernel(cells, packed_ref, fields_ref, wide_ref, out_hbm, factor_hbm,
                          gram, work, out_ref, factor_ref, upper, inverse, sems):
    nb = 4
    lane = lax.broadcasted_iota(jnp.int32, (8, 128), 1)

    def carried(j, row):
        tile = packed_ref[0, 4 * j * (j + 3), row:row + 1, :]
        return jnp.broadcast_to(tile, (8, 128))

    turned = pltpu.roll(carried(0, 2), 64, 1)
    squared = jnp.where(lane < 64, turned, carried(0, 2))[0:1]
    aligned = [jnp.where(lane < 64, pltpu.roll(carried(j, 1), 64, 1), carried(j, 0))[0:1] for j in range(nb)]
    weight = [a / (squared + EPSILON) for a in aligned]
    ratio = jnp.sqrt(squared + 2 * EPSILON) / (squared + EPSILON)
    removed = [a * ratio for a in aligned]

    def span(j):
        return slice(128 * j, 128 * j + 128)

    def prepare(i, j):
        b = i * (i + 1) // 2 + j
        tall = jnp.broadcast_to(removed[i], (128, 128)).T
        raw = packed_ref[:, 8 * b:8 * b + 8].reshape(128, 128)
        if i == j:
            top = jnp.where(lane < 64, raw[:8], raw.T[:8])
            raw = jnp.concatenate([top, raw[8:]], axis=0)
        gram[span(i), span(j)] = (raw - tall * removed[j]) * (1.0 / cells)
        if i != j:
            factor_ref[span(j), span(i)] = jnp.zeros((128, 128), jnp.float32)

    def project(i, j):
        work[span(i), span(j)] = fields_ref[span(i), span(j)] - wide_ref[span(i)] * weight[j]

    def panel(i, j):
        factor_ref[span(i), span(j)] = dot_nt(gram[span(i), span(j)], inverse[j])

    def update(i, k, j):
        gram[span(i), span(k)] = gram[span(i), span(k)] - dot_nt(factor_ref[span(i), span(j)],
                                                                factor_ref[span(k), span(j)])

    def result(c, j):
        out_ref[span(c), span(j)] = dot_nt(work[span(c), span(j)], inverse[j])

    def remove(c, k, j):
        work[span(c), span(k)] = work[span(c), span(k)] - dot_nt(out_ref[span(c), span(j)],
                                                                factor_ref[span(k), span(j)])

    def sent(j):
        here = pl.ds(128 * j, 128)
        return pltpu.make_async_copy(out_ref.at[:, here], out_hbm.at[:, here], sems.at[j])

    factor_copy = pltpu.make_async_copy(factor_ref, factor_hbm, sems.at[nb])
    prepare(0, 0)
    aside = [functools.partial(prepare, i, j) for i in range(1, nb) for j in range(i + 1)]
    aside += [functools.partial(project, i, j) for j in range(nb) for i in range(nb)]
    for j in range(nb):
        factor_diagonal(gram.at[span(j), span(j)], upper, inverse.at[j], aside)
        factor_ref[span(j), span(j)] = upper[...].T
        aside = []
        if j + 1 < nb:
            panel(j + 1, j)
            update(j + 1, j + 1, j)
            aside += [functools.partial(panel, i, j) for i in range(j + 2, nb)]
            aside += [functools.partial(update, i, k, j) for i in range(j + 2, nb) for k in range(j + 1, i + 1)]
            aside += [functools.partial(result, c, j) for c in range(nb)]
            aside += [sent(j).start]
            aside += [functools.partial(remove, c, k, j) for k in range(j + 1, nb) for c in range(nb)]
    factor_copy.start()
    for c in range(nb):
        result(c, nb - 1)
    sent(nb - 1).start()
    for j in range(nb):
        sent(j).wait()
    factor_copy.wait()


def orthonormalize(packed, fields, wide, cells):
    n = fields.shape[0]
    vm = pl.BlockSpec(memory_space=pltpu.VMEM)
    hbm = pl.BlockSpec(memory_space=pltpu.HBM)
    return pl.pallas_call(
        functools.partial(orthonormalize_kernel, cells),
        out_shape=(jax.ShapeDtypeStruct((n, 512), jnp.float32), jax.ShapeDtypeStruct((512, 512), jnp.float32)),
        in_specs=[vm] * 3, out_specs=(hbm, hbm),
        scratch_shapes=[pltpu.VMEM((512, 512), jnp.float32), pltpu.VMEM((n, 512), jnp.float32),
                        pltpu.VMEM((n, 512), jnp.float32), pltpu.VMEM((512, 512), jnp.float32),
                        pltpu.VMEM((128, 128), jnp.float32), pltpu.VMEM((4, 128, 128), jnp.float32),
                        pltpu.SemaphoreType.DMA((5,))],
        compiler_params=pltpu.CompilerParams(vmem_limit_bytes=40 * 1024 * 1024),
    )(packed, fields, wide)


MESH = pl.DeviceIdType.MESH
TILES = 80
HALF = 40
PIECE = 5
LEVEL_OF_ROUND = (2, 1, 1, 0)


def evolve_kernel(fields_hbm, tables_hbm, evolved_ref, out_ref, wide_ref,
                  fields_ref, tables_ref,
                  coef, trial, late, slope, x_send, y_send, x_recv, y_recv,
                  pack, from_core, mid, from_plane, tail, from_ring,
                  in_sems, x_sems, y_sems, core_sems, plane_sems, ring_sems, back_sems):
    gx, gy = lax.axis_index("gx"), lax.axis_index("gy")
    core, y = lax.rem(gx, 2), lax.div(gx, 2)
    z, x = lax.rem(gy, 8), lax.div(gy, 8)
    other = 1 - core
    partner = (gx + 1 - 2 * core, gy)
    x_sides = ((lax.rem(gx + 1, 8), gy), (lax.rem(gx + 7, 8), gy))
    y_sides = ((gx, lax.rem(gy + 1, 32)), (gx, lax.rem(gy + 31, 32)))

    def on_plane(offset):
        peer_y, peer_x = lax.rem(y + offset[0], 4), lax.rem(x + offset[1], 4)
        return place_of(peer_y, peer_x), (2 * peer_y + core, 8 * peer_x + z)

    def place_of(at_y, at_x):
        return 8 * lax.rem(at_y + at_x, 2) + 2 * at_y + lax.div(at_x, 2)

    offsets = sorted(((a, b) for a in range(4) for b in range(4) if a or b),
                     key=lambda o: -(min(o[0], 4 - o[0]) + min(o[1], 4 - o[1])))
    place = place_of(y, x)

    def along_z(step):
        peer = lax.rem(z + step, 8)
        return peer, (gx, 8 * x + peer)

    barrier = pltpu.get_barrier_semaphore()
    greeted = [*x_sides, *y_sides, partner]
    greeted += [on_plane(offset)[1] for offset in offsets]
    greeted += [along_z(step)[1] for step in range(1, 8)]
    for device in greeted:
        pl.semaphore_signal(barrier, inc=1, device_id=device, device_id_type=MESH)
    loads = [pltpu.make_async_copy(tables_hbm, tables_ref, in_sems.at[4])]
    for g in range(4):
        lanes = pl.ds(128 * g, 128)
        loads.append(pltpu.make_async_copy(fields_hbm.at[:, :, :, lanes], fields_ref.at[:, :, :, lanes],
                                           in_sems.at[g]))
    for load in loads:
        load.start()

    def spread(level):
        depth = lax.broadcasted_iota(jnp.int32, (16, 128), 0)
        for component in range(7):
            if component == 0:
                table = tables_ref[32 * level:32 * level + 32, :].T
            else:
                start = 96 + 192 * level + 32 * (component - 1)
                table = tables_ref[start:start + 32, :].T
            for cell in range(32):
                value = jnp.broadcast_to(table[:, cell:cell + 1], (16, 128))
                if component == 5:
                    value = jnp.where(depth == 15, 0.0, value)
                if component == 6:
                    value = jnp.where(depth == 0, 0.0, value)
                coef[level, component, cell // 8, cell % 8] = value

    def lanes_of(g):
        return slice(128 * g, 128 * g + 128)

    def held(r, g, i):
        if r == 0:
            return fields_ref[i, :, :, lanes_of(g)]
        if r == 2:
            return evolved_ref[128 * i:128 * i + 128, lanes_of(g)].reshape(8, 16, 128)
        return trial[g, i]

    def face_copies(r, g):
        copies = []
        for side in range(2):
            copies.append(pltpu.make_async_remote_copy(
                src_ref=x_send.at[r, g, side], dst_ref=x_recv.at[r, g, side],
                send_sem=x_sems.at[0, r, g, side], recv_sem=x_sems.at[1, r, g, side],
                device_id=x_sides[side], device_id_type=MESH))
            copies.append(pltpu.make_async_remote_copy(
                src_ref=y_send.at[r, g, side], dst_ref=y_recv.at[r, g, side],
                send_sem=y_sems.at[0, r, g, side], recv_sem=y_sems.at[1, r, g, side],
                device_id=y_sides[side], device_id_type=MESH))
        return copies

    def send_faces(r, g):
        level = LEVEL_OF_ROUND[r]
        copies = face_copies(r, g)
        x_edge = (gx < 7, gx > 0)
        y_edge = (gy < 31, gy > 0)
        for side in range(2):
            j = (7, 0)[side]
            for i in range(4):
                value = held(r, g, i)[j]
                y_send[r, g, side, i] = jnp.where(y_edge[side], coef[level, 3 + side, i, j] * value, 0.0)
            copies[2 * side + 1].start()
        for side in range(2):
            i = (3, 0)[side]
            x_send[r, g, side] = jnp.where(x_edge[side], coef[level, 1 + side, i] * held(r, g, i), 0.0)
            copies[2 * side].start()

    def local_terms(r, g):
        level = LEVEL_OF_ROUND[r]
        for i in range(4):
            v = held(r, g, i)
            total = coef[level, 0, i] * v
            up = (coef[level, 5, i] * v).reshape(128, 128)
            down = (coef[level, 6, i] * v).reshape(128, 128)
            total = total + pltpu.roll(up, 1, 0).reshape(8, 16, 128)
            total = total + pltpu.roll(down, 127, 0).reshape(8, 16, 128)
            if i > 0:
                total = total + coef[level, 1, i - 1] * held(r, g, i - 1)
            if i < 3:
                total = total + coef[level, 2, i + 1] * held(r, g, i + 1)
            zero = jnp.zeros((1, 16, 128), jnp.float32)
            total = total + jnp.concatenate([zero, (coef[level, 3, i] * v)[:7]], axis=0)
            total = total + jnp.concatenate([(coef[level, 4, i] * v)[1:], zero], axis=0)
            slope[g, i] = total

    def finish(r, g):
        parts = []
        for c in face_copies(r, g):
            c.wait()
        for i in range(4):
            total = slope[g, i]
            if i == 0:
                total = total + x_recv[r, g, 0]
            if i == 3:
                total = total + x_recv[r, g, 1]
            total = jnp.concatenate([(total[0] + y_recv[r, g, 0, i])[None], total[1:7],
                                     (total[7] + y_recv[r, g, 1, i])[None]], axis=0)
            start = held(0 if r < 2 else 2, g, i)
            if r % 2 == 0:
                late[g, i] = total
                trial[g, i] = start + STEP_SIZE * total
            else:
                done = start + 0.5 * STEP_SIZE * (late[g, i] + total)
                evolved_ref[128 * i:128 * i + 128, lanes_of(g)] = done.reshape(128, 128)
                if r == 3:
                    parts.append(jnp.sum(done.reshape(16, 8, 128) * wide_ref[128 * i:128 * i + 128].reshape(16, 8, 128),
                                         axis=0))
        return parts

    def copy(src, dst, sems, mine, theirs, device):
        return pltpu.make_async_remote_copy(src_ref=src, dst_ref=dst, send_sem=sems.at[0, theirs],
                                            recv_sem=sems.at[1, mine], device_id=device, device_id_type=MESH)

    def core_copy(b):
        span = pl.ds(8 * b, 8)
        return copy(pack.at[other, span], from_core.at[span], core_sems, b, b, partner)

    def plane_start(wave):
        for offset in offsets:
            peer, device = on_plane(offset)

            @pl.when(lax.div(peer, 8) == wave)
            def _():
                copy(mid.at[pl.ds(peer * PIECE, PIECE)], from_plane.at[place], plane_sems, place, peer,
                     device).start()

    loads[0].wait()
    spread(2)
    pl.semaphore_wait(barrier, len(greeted))
    for r in range(4):
        for g in range(4):
            if r > 0:
                finish(r - 1, g)
            else:
                loads[1 + g].wait()
            send_faces(r, g)
            local_terms(r, g)
        if r < 2:
            spread(1 - r)
        if r == 2:
            table = tables_ref[672:704].T
            for cell in range(32):
                wide_ref[16 * cell:16 * cell + 16] = jnp.broadcast_to(table[:, cell:cell + 1], (16, 128))

    sub = lax.broadcasted_iota(jnp.int32, (8, 128), 0)
    lane = lax.broadcasted_iota(jnp.int32, (8, 128), 1)
    squared = jnp.sum(tables_ref[672:704] * tables_ref[672:704])
    for g in range(4):
        parts = finish(3, g)
        product = lax.dot_general(evolved_ref[:, lanes_of(g)], evolved_ref[:, :128 * g + 128],
                                  (((0,), (0,)), ((), ())), precision=HIGHEST,
                                  preferred_element_type=jnp.float32)
        for j in range(g + 1):
            b = g * (g + 1) // 2 + j
            pack[:, 8 * b:8 * b + 8] = product[:, 128 * j:128 * j + 128].reshape(2, 8, 8, 128)
            if j == g:
                aligned = jnp.sum(parts[0] + parts[1] + (parts[2] + parts[3]), axis=0, keepdims=True)
                aligned = jnp.broadcast_to(aligned, (8, 128))
                carried = jnp.where(sub == 0, aligned, jnp.where(sub == 1, pltpu.roll(aligned, 64, 1), squared))
                pack[0, 8 * b] = jnp.where((lane >= 64) & (sub < 3), carried, product[:8, 128 * j:128 * j + 128])
            core_copy(b).start()
        if g == 2:
            for b in range(5):
                core_copy(b).wait()
            mid[0:HALF] = pack[core, 0:HALF] + from_core[0:HALF]
            plane_start(0)
    for b in range(5, 10):
        core_copy(b).wait()
    mid[HALF:TILES] = pack[core, HALF:TILES] + from_core[HALF:TILES]
    plane_start(1)

    total = mid[pl.ds(place * PIECE, PIECE)]
    for offset in reversed(offsets):
        peer, device = on_plane(offset)
        copy(mid.at[pl.ds(peer * PIECE, PIECE)], from_plane.at[peer], plane_sems, peer, peer, device).wait()
        total = total + from_plane[peer]
    tail[...] = total
    for step in (4, 3, 5, 2, 6, 1, 7):
        peer, device = along_z(step)
        copy(tail, from_ring.at[z], ring_sems, z, peer, device).start()
    from_ring[z] = total
    for step in (1, 7, 2, 6, 3, 5, 4):
        peer, device = along_z(step)
        copy(tail, from_ring.at[peer], ring_sems, peer, peer, device).wait()
    final = from_ring[0]
    for p in range(1, 8):
        final = final + from_ring[p]

    def back(side, owner, device):
        spot = out_ref.at[side, pl.ds(owner * PIECE, PIECE)]
        return copy(spot, spot, back_sems, owner, owner, device)

    def forward(side, owner):
        spot = out_ref.at[side, pl.ds(owner * PIECE, PIECE)]
        return copy(spot, spot, back_sems, 16 + owner, 16 + owner, partner)

    out_ref[core, pl.ds(place * PIECE, PIECE)] = final
    for offset in offsets:
        peer, device = on_plane(offset)
        spot = out_ref.at[core, pl.ds(place * PIECE, PIECE)]
        copy(spot, spot, back_sems, place, peer, device).start()
    forward(core, place).start()
    for offset in reversed(offsets):
        peer, device = on_plane(offset)
        back(core, peer, device).wait()
        forward(core, peer).start()
    for owner in range(16):
        forward(other, owner).wait()


def evolve_and_reduce(fields, tables):
    vm = pl.BlockSpec(memory_space=pltpu.VMEM)
    hbm = pl.BlockSpec(memory_space=pltpu.HBM)

    def tiles(*lead):
        return pltpu.VMEM((*lead, 8, 128), jnp.float32)

    def columns(*lead):
        return pltpu.VMEM((*lead, 16, 128), jnp.float32)

    arguments = (fields, tables)
    return pl.pallas_call(
        evolve_kernel,
        out_shape=(jax.ShapeDtypeStruct((512, 512), jnp.float32),
                   jax.ShapeDtypeStruct((2, TILES, 8, 128), jnp.float32),
                   jax.ShapeDtypeStruct((512, 128), jnp.float32)),
        in_specs=[hbm] * 2, out_specs=(vm, vm, vm),
        scratch_shapes=[
            *[pltpu.VMEM(a.shape, jnp.float32) for a in arguments],
            columns(3, 7, 4, 8), columns(4, 4, 8), columns(4, 4, 8), columns(4, 4, 8),
            columns(4, 4, 2, 8), columns(4, 4, 2, 4), columns(4, 4, 2, 8), columns(4, 4, 2, 4),
            tiles(2, TILES), tiles(TILES), tiles(TILES), tiles(16, PIECE), tiles(PIECE), tiles(8, PIECE),
            pltpu.SemaphoreType.DMA((5,)),
            pltpu.SemaphoreType.DMA((2, 4, 4, 2)), pltpu.SemaphoreType.DMA((2, 4, 4, 2)),
            pltpu.SemaphoreType.DMA((2, 10)), pltpu.SemaphoreType.DMA((2, 16)),
            pltpu.SemaphoreType.DMA((2, 8)), pltpu.SemaphoreType.DMA((2, 32)),
        ],
        compiler_params=pltpu.CompilerParams(collective_id=1, has_side_effects=True,
                                             vmem_limit_bytes=103 * 512 * 1024),
    )(*arguments)


def shards(adjoint_fields, center_coef, neighbor_coef, neutral):
    cells_x, cells_y, depth_cells, columns = adjoint_fields.shape
    cell_count = cells_x * lax.axis_size("gx") * cells_y * lax.axis_size("gy") * depth_cells
    tables = jnp.concatenate([a.reshape(-1, depth_cells) for a in (center_coef, neighbor_coef, neutral)], axis=0)
    evolved, packed, wide = evolve_and_reduce(adjoint_fields, tables)
    orthonormal, factor = orthonormalize(packed, evolved, wide, cell_count)
    return (orthonormal.reshape(adjoint_fields.shape), factor)


def solution(mesh):
    in_specs = (
        P("gx", "gy", None, None),
        P(None, "gx", "gy", None),
        P(None, None, "gx", "gy", None),
        P("gx", "gy", None),
    )
    out_specs = (P("gx", "gy", None, None), P())
    return jax.shard_map(shards, mesh=mesh, in_specs=in_specs, out_specs=out_specs, check_vma=False)
```

```python
import functools

import jax
import jax.numpy as jnp
from jax import lax
from jax.experimental import pallas as pl
from jax.experimental.pallas import tpu as pltpu
from jax.sharding import PartitionSpec as P

STEP_SIZE = 0.15
EPSILON = 1e-06
HIGHEST = lax.Precision.HIGHEST


def dot_nt(a, b):
    return lax.dot_general(a, b, (((1,), (1,)), ((), ())), precision=HIGHEST,
                           preferred_element_type=jnp.float32)


def lanes(value, column):
    return jnp.broadcast_to(value[:, column:column + 1], (8, 128))


def rows(value, row):
    return jnp.broadcast_to(value[row:row + 1, :], (8, 128))


def three_parts(value):
    high = value.astype(jnp.bfloat16).astype(jnp.float32)
    rest = value - high
    middle = rest.astype(jnp.bfloat16).astype(jnp.float32)
    return high, middle, rest - middle


def outer_product(value):
    h, m, l = three_parts(value)
    tall = jnp.concatenate([h, h, m, h, l, m], axis=0).astype(jnp.bfloat16)
    wide = jnp.concatenate([h, m, h, l, h, m], axis=0).astype(jnp.bfloat16)
    return lax.dot_general(tall, wide, (((0,), (0,)), ((), ())), preferred_element_type=jnp.float32)


NEAR = 2
FEW = 3


def invert_factor(block_ref, inverse_ref, aside):
    sub = lax.broadcasted_iota(jnp.int32, (8, 128), 0)
    lane = lax.broadcasted_iota(jnp.int32, (8, 128), 1)
    left = [block_ref[8 * i:8 * i + 8, :] for i in range(16)]
    columns = [lanes(left[0], r) for r in range(8)]
    for k in range(16):
        base = 8 * k
        pivot = (lane >= base) & (lane < base + 8)
        entry = {(q, r): rows(columns[r], q) for r in range(8) for q in range(r, 8)}
        mine = jnp.where(pivot, jnp.where(lane == sub + base, 1.0, 0.0), left[k])
        u = [rows(mine, r) for r in range(8)]
        scale = []
        lower = {}
        for r in range(8):
            s = lax.rsqrt(entry[r, r])
            scale.append(s)
            for q in range(r + 1, 8):
                lower[q, r] = entry[q, r] * s
            for q in range(r + 1, 8):
                for t in range(r + 1, q + 1):
                    entry[q, t] = entry[q, t] - lower[q, r] * lower[t, r]
            u[r] = u[r] * s
            for q in range(r + 1, 8):
                u[q] = u[q] - lower[q, r] * u[r]
        up = u[0]
        for r in range(1, 8):
            up = jnp.where(sub == r, u[r], up)
        inverse_ref[base:base + 8, :] = jnp.where(lane < base + 8, up, 0.0)
        near = min(16, k + 1 + NEAR)
        if 16 - near < FEW:
            near = 16
        for i in range(k + 1, near):
            col = [lanes(left[i], base + r) for r in range(8)]
            if i == k + 1:
                after = [lanes(left[i], base + 8 + r) for r in range(8)]
            for r in range(8):
                col[r] = col[r] * scale[r]
                for q in range(r + 1, 8):
                    col[q] = col[q] - lower[q, r] * col[r]
            if i == k + 1:
                for r in range(8):
                    for t in range(8):
                        after[t] = after[t] - col[r] * rows(col[r], t)
                columns = after
            left[i] = jnp.where(pivot, 0.0, left[i])
            for r in range(8):
                left[i] = left[i] - col[r] * u[r]
        if near < 16:
            delta = outer_product(up)
            for i in range(near, 16):
                left[i] = jnp.where(pivot, 0.0, left[i]) - delta[8 * i:8 * i + 8, :]
        for work in aside[len(aside) * k // 15:len(aside) * (k + 1) // 15]:
            work()


def orthonormalize_kernel(cells, packed_ref, fields_ref, wide_ref, out_hbm, factor_hbm,
                          gram, work, out_ref, factor_ref, inverse, sems):
    nb = 4
    lane = lax.broadcasted_iota(jnp.int32, (8, 128), 1)

    def carried(j, row):
        tile = packed_ref[0, 4 * j * (j + 3), row:row + 1, :]
        return jnp.broadcast_to(tile, (8, 128))

    turned = pltpu.roll(carried(0, 2), 64, 1)
    squared = jnp.where(lane < 64, turned, carried(0, 2))[0:1]
    aligned = [jnp.where(lane < 64, pltpu.roll(carried(j, 1), 64, 1), carried(j, 0))[0:1] for j in range(nb)]
    weight = [a / (squared + EPSILON) for a in aligned]
    ratio = jnp.sqrt(squared + 2 * EPSILON) / (squared + EPSILON)
    removed = [a * ratio for a in aligned]

    def span(j):
        return slice(128 * j, 128 * j + 128)

    def prepare(i, j):
        b = i * (i + 1) // 2 + j
        tall = jnp.broadcast_to(removed[i], (128, 128)).T
        raw = packed_ref[:, 8 * b:8 * b + 8].reshape(128, 128)
        if i == j:
            top = jnp.where(lane < 64, raw[:8], raw.T[:8])
            raw = jnp.concatenate([top, raw[8:]], axis=0)
        gram[span(i), span(j)] = (raw - tall * removed[j]) * (1.0 / cells)
        if i != j:
            factor_ref[span(j), span(i)] = jnp.zeros((128, 128), jnp.float32)

    def project(i, j):
        work[span(i), span(j)] = fields_ref[span(i), span(j)] - wide_ref[span(i)] * weight[j]

    def panel(i, j):
        factor_ref[span(i), span(j)] = dot_nt(gram[span(i), span(j)], inverse[j])

    def diagonal(j):
        row = lax.broadcasted_iota(jnp.int32, (128, 128), 0)
        column = lax.broadcasted_iota(jnp.int32, (128, 128), 1)
        product = dot_nt(gram[span(j), span(j)], inverse[j])
        factor_ref[span(j), span(j)] = jnp.where(row >= column, product, 0.0)

    def update(i, k, j):
        gram[span(i), span(k)] = gram[span(i), span(k)] - dot_nt(factor_ref[span(i), span(j)],
                                                                factor_ref[span(k), span(j)])

    def result(c, j):
        out_ref[span(c), span(j)] = dot_nt(work[span(c), span(j)], inverse[j])

    def remove(c, k, j):
        work[span(c), span(k)] = work[span(c), span(k)] - dot_nt(out_ref[span(c), span(j)],
                                                                factor_ref[span(k), span(j)])

    def sent(j):
        here = pl.ds(128 * j, 128)
        return pltpu.make_async_copy(out_ref.at[:, here], out_hbm.at[:, here], sems.at[j])

    factor_copy = pltpu.make_async_copy(factor_ref, factor_hbm, sems.at[nb])
    prepare(0, 0)
    aside = [functools.partial(prepare, i, j) for i in range(1, nb) for j in range(i + 1)]
    aside += [functools.partial(project, i, j) for j in range(nb) for i in range(nb)]
    for j in range(nb):
        invert_factor(gram.at[span(j), span(j)], inverse.at[j], aside)
        aside = [functools.partial(diagonal, j)]
        if j + 1 < nb:
            panel(j + 1, j)
            update(j + 1, j + 1, j)
            aside += [functools.partial(panel, i, j) for i in range(j + 2, nb)]
            aside += [functools.partial(update, i, k, j) for i in range(j + 2, nb) for k in range(j + 1, i + 1)]
            aside += [functools.partial(result, c, j) for c in range(nb)]
            aside += [sent(j).start]
            aside += [functools.partial(remove, c, k, j) for k in range(j + 1, nb) for c in range(nb)]
    for c in range(nb):
        result(c, nb - 1)
    sent(nb - 1).start()
    diagonal(nb - 1)
    factor_copy.start()
    for j in range(nb):
        sent(j).wait()
    factor_copy.wait()


def orthonormalize(packed, fields, wide, cells):
    n = fields.shape[0]
    vm = pl.BlockSpec(memory_space=pltpu.VMEM)
    hbm = pl.BlockSpec(memory_space=pltpu.HBM)
    return pl.pallas_call(
        functools.partial(orthonormalize_kernel, cells),
        out_shape=(jax.ShapeDtypeStruct((n, 512), jnp.float32), jax.ShapeDtypeStruct((512, 512), jnp.float32)),
        in_specs=[vm] * 3, out_specs=(hbm, hbm),
        scratch_shapes=[pltpu.VMEM((512, 512), jnp.float32), pltpu.VMEM((n, 512), jnp.float32),
                        pltpu.VMEM((n, 512), jnp.float32), pltpu.VMEM((512, 512), jnp.float32),
                        pltpu.VMEM((4, 128, 128), jnp.float32),
                        pltpu.SemaphoreType.DMA((5,))],
        compiler_params=pltpu.CompilerParams(vmem_limit_bytes=40 * 1024 * 1024),
    )(packed, fields, wide)


MESH = pl.DeviceIdType.MESH
TILES = 80
HALF = 40
PIECE = 5
LEVEL_OF_ROUND = (2, 1, 1, 0)


def evolve_kernel(fields_hbm, tables_ref, evolved_ref, out_ref, wide_ref,
                  fields_ref,
                  coef, trial, late, slope, x_send, y_send, x_recv, y_recv,
                  pack, from_core, mid, from_plane, tail, from_ring,
                  in_sems, x_sems, y_sems, core_sems, plane_sems, ring_sems, back_sems):
    gx, gy = lax.axis_index("gx"), lax.axis_index("gy")
    core, y = lax.rem(gx, 2), lax.div(gx, 2)
    z, x = lax.rem(gy, 8), lax.div(gy, 8)
    other = 1 - core
    partner = (gx + 1 - 2 * core, gy)
    x_sides = ((lax.rem(gx + 1, 8), gy), (lax.rem(gx + 7, 8), gy))
    y_sides = ((gx, lax.rem(gy + 1, 32)), (gx, lax.rem(gy + 31, 32)))

    def on_plane(offset):
        peer_y, peer_x = lax.rem(y + offset[0], 4), lax.rem(x + offset[1], 4)
        return place_of(peer_y, peer_x), (2 * peer_y + core, 8 * peer_x + z)

    def place_of(at_y, at_x):
        return 8 * lax.rem(at_y + at_x, 2) + 2 * at_y + lax.div(at_x, 2)

    offsets = sorted(((a, b) for a in range(4) for b in range(4) if a or b),
                     key=lambda o: -(min(o[0], 4 - o[0]) + min(o[1], 4 - o[1])))
    place = place_of(y, x)

    def along_z(step):
        peer = lax.rem(z + step, 8)
        return peer, (gx, 8 * x + peer)

    barrier = pltpu.get_barrier_semaphore()
    greeted = [*x_sides, *y_sides, partner]
    greeted += [on_plane(offset)[1] for offset in offsets]
    greeted += [along_z(step)[1] for step in range(1, 8)]
    for device in greeted:
        pl.semaphore_signal(barrier, inc=1, device_id=device, device_id_type=MESH)
    loads = []
    for g in range(4):
        lanes = pl.ds(128 * g, 128)
        loads.append(pltpu.make_async_copy(fields_hbm.at[:, :, :, lanes], fields_ref.at[:, :, :, lanes],
                                           in_sems.at[g]))
    for load in loads:
        load.start()

    def spread(level):
        depth = lax.broadcasted_iota(jnp.int32, (16, 128), 0)
        for component in range(7):
            if component == 0:
                table = tables_ref[32 * level:32 * level + 32, :].T
            else:
                start = 96 + 192 * level + 32 * (component - 1)
                table = tables_ref[start:start + 32, :].T
            for cell in range(32):
                value = jnp.broadcast_to(table[:, cell:cell + 1], (16, 128))
                if component == 5:
                    value = jnp.where(depth == 15, 0.0, value)
                if component == 6:
                    value = jnp.where(depth == 0, 0.0, value)
                coef[level, component, cell // 8, cell % 8] = value

    def lanes_of(g):
        return slice(128 * g, 128 * g + 128)

    def held(r, g, i):
        if r == 0:
            return fields_ref[i, :, :, lanes_of(g)]
        if r == 2:
            return evolved_ref[128 * i:128 * i + 128, lanes_of(g)].reshape(8, 16, 128)
        return trial[g, i]

    def face_copies(r, g):
        copies = []
        for side in range(2):
            copies.append(pltpu.make_async_remote_copy(
                src_ref=x_send.at[r, g, side], dst_ref=x_recv.at[r, g, side],
                send_sem=x_sems.at[0, r, g, side], recv_sem=x_sems.at[1, r, g, side],
                device_id=x_sides[side], device_id_type=MESH))
            copies.append(pltpu.make_async_remote_copy(
                src_ref=y_send.at[r, g, side], dst_ref=y_recv.at[r, g, side],
                send_sem=y_sems.at[0, r, g, side], recv_sem=y_sems.at[1, r, g, side],
                device_id=y_sides[side], device_id_type=MESH))
        return copies

    def send_faces(r, g):
        level = LEVEL_OF_ROUND[r]
        copies = face_copies(r, g)
        x_edge = (gx < 7, gx > 0)
        y_edge = (gy < 31, gy > 0)
        for side in range(2):
            j = (7, 0)[side]
            for i in range(4):
                value = held(r, g, i)[j]
                y_send[r, g, side, i] = jnp.where(y_edge[side], coef[level, 3 + side, i, j] * value, 0.0)
            if (r, g, side) == (0, 0, 0):
                pl.semaphore_wait(barrier, len(greeted))
            copies[2 * side + 1].start()
        for side in range(2):
            i = (3, 0)[side]
            x_send[r, g, side] = jnp.where(x_edge[side], coef[level, 1 + side, i] * held(r, g, i), 0.0)
            copies[2 * side].start()

    def local_terms(r, g):
        level = LEVEL_OF_ROUND[r]
        for i in range(4):
            v = held(r, g, i)
            total = coef[level, 0, i] * v
            up = (coef[level, 5, i] * v).reshape(128, 128)
            down = (coef[level, 6, i] * v).reshape(128, 128)
            total = total + pltpu.roll(up, 1, 0).reshape(8, 16, 128)
            total = total + pltpu.roll(down, 127, 0).reshape(8, 16, 128)
            if i > 0:
                total = total + coef[level, 1, i - 1] * held(r, g, i - 1)
            if i < 3:
                total = total + coef[level, 2, i + 1] * held(r, g, i + 1)
            zero = jnp.zeros((1, 16, 128), jnp.float32)
            total = total + jnp.concatenate([zero, (coef[level, 3, i] * v)[:7]], axis=0)
            total = total + jnp.concatenate([(coef[level, 4, i] * v)[1:], zero], axis=0)
            slope[g, i] = total

    def finish(r, g):
        parts = []
        for c in face_copies(r, g):
            c.wait()
        for i in range(4):
            total = slope[g, i]
            if i == 0:
                total = total + x_recv[r, g, 0]
            if i == 3:
                total = total + x_recv[r, g, 1]
            total = jnp.concatenate([(total[0] + y_recv[r, g, 0, i])[None], total[1:7],
                                     (total[7] + y_recv[r, g, 1, i])[None]], axis=0)
            start = held(0 if r < 2 else 2, g, i)
            if r % 2 == 0:
                late[g, i] = total
                trial[g, i] = start + STEP_SIZE * total
            else:
                done = start + 0.5 * STEP_SIZE * (late[g, i] + total)
                evolved_ref[128 * i:128 * i + 128, lanes_of(g)] = done.reshape(128, 128)
                if r == 3:
                    parts.append(jnp.sum(done.reshape(16, 8, 128) * wide_ref[128 * i:128 * i + 128].reshape(16, 8, 128),
                                         axis=0))
        return parts

    def copy(src, dst, sems, mine, theirs, device):
        return pltpu.make_async_remote_copy(src_ref=src, dst_ref=dst, send_sem=sems.at[0, theirs],
                                            recv_sem=sems.at[1, mine], device_id=device, device_id_type=MESH)

    def core_copy(b):
        span = pl.ds(8 * b, 8)
        return copy(pack.at[other, span], from_core.at[span], core_sems, b, b, partner)

    def plane_start(wave):
        for offset in offsets:
            peer, device = on_plane(offset)

            @pl.when(lax.div(peer, 8) == wave)
            def _():
                copy(mid.at[pl.ds(peer * PIECE, PIECE)], from_plane.at[place], plane_sems, place, peer,
                     device).start()

    spread(2)
    for r in range(4):
        for g in range(4):
            if r > 0:
                finish(r - 1, g)
            else:
                loads[g].wait()
            send_faces(r, g)
            local_terms(r, g)
        if r < 2:
            spread(1 - r)
        if r == 2:
            table = tables_ref[672:704].T
            for cell in range(32):
                wide_ref[16 * cell:16 * cell + 16] = jnp.broadcast_to(table[:, cell:cell + 1], (16, 128))

    sub = lax.broadcasted_iota(jnp.int32, (8, 128), 0)
    lane = lax.broadcasted_iota(jnp.int32, (8, 128), 1)
    squared = jnp.sum(tables_ref[672:704] * tables_ref[672:704])
    for g in range(4):
        parts = finish(3, g)
        product = lax.dot_general(evolved_ref[:, lanes_of(g)], evolved_ref[:, :128 * g + 128],
                                  (((0,), (0,)), ((), ())), precision=HIGHEST,
                                  preferred_element_type=jnp.float32)
        for j in range(g + 1):
            b = g * (g + 1) // 2 + j
            pack[:, 8 * b:8 * b + 8] = product[:, 128 * j:128 * j + 128].reshape(2, 8, 8, 128)
            if j == g:
                aligned = jnp.sum(parts[0] + parts[1] + (parts[2] + parts[3]), axis=0, keepdims=True)
                aligned = jnp.broadcast_to(aligned, (8, 128))
                carried = jnp.where(sub == 0, aligned, jnp.where(sub == 1, pltpu.roll(aligned, 64, 1), squared))
                pack[0, 8 * b] = jnp.where((lane >= 64) & (sub < 3), carried, product[:8, 128 * j:128 * j + 128])
            core_copy(b).start()
        if g == 2:
            for b in range(5):
                core_copy(b).wait()
            mid[0:HALF] = pack[core, 0:HALF] + from_core[0:HALF]
            plane_start(0)
    for b in range(5, 10):
        core_copy(b).wait()
    mid[HALF:TILES] = pack[core, HALF:TILES] + from_core[HALF:TILES]
    plane_start(1)

    total = mid[pl.ds(place * PIECE, PIECE)]
    for offset in reversed(offsets):
        peer, device = on_plane(offset)
        copy(mid.at[pl.ds(peer * PIECE, PIECE)], from_plane.at[peer], plane_sems, peer, peer, device).wait()
        total = total + from_plane[peer]
    tail[...] = total
    for step in (4, 3, 5, 2, 6, 1, 7):
        peer, device = along_z(step)
        copy(tail, from_ring.at[z], ring_sems, z, peer, device).start()
    from_ring[z] = total
    for step in (1, 7, 2, 6, 3, 5, 4):
        peer, device = along_z(step)
        copy(tail, from_ring.at[peer], ring_sems, peer, peer, device).wait()
    final = from_ring[0]
    for p in range(1, 8):
        final = final + from_ring[p]

    def back(side, owner, device):
        spot = out_ref.at[side, pl.ds(owner * PIECE, PIECE)]
        return copy(spot, spot, back_sems, owner, owner, device)

    def forward(side, owner):
        spot = out_ref.at[side, pl.ds(owner * PIECE, PIECE)]
        return copy(spot, spot, back_sems, 16 + owner, 16 + owner, partner)

    out_ref[core, pl.ds(place * PIECE, PIECE)] = final
    for offset in offsets:
        peer, device = on_plane(offset)
        spot = out_ref.at[core, pl.ds(place * PIECE, PIECE)]
        copy(spot, spot, back_sems, place, peer, device).start()
    forward(core, place).start()
    for offset in reversed(offsets):
        peer, device = on_plane(offset)
        back(core, peer, device).wait()
        forward(core, peer).start()
    for owner in range(16):
        forward(other, owner).wait()


def evolve_and_reduce(fields, tables):
    vm = pl.BlockSpec(memory_space=pltpu.VMEM)
    hbm = pl.BlockSpec(memory_space=pltpu.HBM)

    def tiles(*lead):
        return pltpu.VMEM((*lead, 8, 128), jnp.float32)

    def columns(*lead):
        return pltpu.VMEM((*lead, 16, 128), jnp.float32)

    return pl.pallas_call(
        evolve_kernel,
        out_shape=(jax.ShapeDtypeStruct((512, 512), jnp.float32),
                   jax.ShapeDtypeStruct((2, TILES, 8, 128), jnp.float32),
                   jax.ShapeDtypeStruct((512, 128), jnp.float32)),
        in_specs=[hbm, vm], out_specs=(vm, vm, vm),
        scratch_shapes=[
            pltpu.VMEM(fields.shape, jnp.float32),
            columns(3, 7, 4, 8), columns(4, 4, 8), columns(4, 4, 8), columns(4, 4, 8),
            columns(4, 4, 2, 8), columns(4, 4, 2, 4), columns(4, 4, 2, 8), columns(4, 4, 2, 4),
            tiles(2, TILES), tiles(TILES), tiles(TILES), tiles(16, PIECE), tiles(PIECE), tiles(8, PIECE),
            pltpu.SemaphoreType.DMA((4,)),
            pltpu.SemaphoreType.DMA((2, 4, 4, 2)), pltpu.SemaphoreType.DMA((2, 4, 4, 2)),
            pltpu.SemaphoreType.DMA((2, 10)), pltpu.SemaphoreType.DMA((2, 16)),
            pltpu.SemaphoreType.DMA((2, 8)), pltpu.SemaphoreType.DMA((2, 32)),
        ],
        compiler_params=pltpu.CompilerParams(collective_id=1, has_side_effects=True,
                                             vmem_limit_bytes=103 * 512 * 1024),
    )(fields, tables)


def shards(adjoint_fields, center_coef, neighbor_coef, neutral):
    cells_x, cells_y, depth_cells, columns = adjoint_fields.shape
    cell_count = cells_x * lax.axis_size("gx") * cells_y * lax.axis_size("gy") * depth_cells
    tables = jnp.concatenate([a.reshape(-1, depth_cells) for a in (center_coef, neighbor_coef, neutral)], axis=0)
    evolved, packed, wide = evolve_and_reduce(adjoint_fields, tables)
    orthonormal, factor = orthonormalize(packed, evolved, wide, cell_count)
    return (orthonormal.reshape(adjoint_fields.shape), factor)


def solution(mesh):
    in_specs = (
        P("gx", "gy", None, None),
        P(None, "gx", "gy", None),
        P(None, None, "gx", "gy", None),
        P("gx", "gy", None),
    )
    out_specs = (P("gx", "gy", None, None), P())
    return jax.shard_map(shards, mesh=mesh, in_specs=in_specs, out_specs=out_specs, check_vma=False)
```
